32 devices in a mesh: scen: 2 (over y), gx: 4 (over z), gy: 4 (over x, core).
Axes of the slice: x: 2, y: 2, z: 4, core: 2. Of those that a mesh axis runs over, the one named last changes fastest.
Arguments:
- head_old: float32 [80, 64, 512], P('scen', 'gx', 'gy'), parts along dimension 0, may hold values from -3 to 1
- soil_class: int32 [40, 64, 512], P(None, 'gx', 'gy'), may hold values from 0 to 11
- ksat_table: float32 [12], replicated, may hold values from 0.05 to 2
- alpha_table: float32 [12], replicated, may hold values from 0.3 to 2
- capacity_table: float32 [12], replicated, may hold values from 0.2 to 2
- rain: float32 [128, 512], P(('scen', 'gx'), 'gy'), parts along dimension 0, may hold values from 0.1 to 2
- lake_level: float32 [128], P('scen'), parts along dimension 0, may hold values from 0 to 2
- pit_id: int32 [64, 512], P('gx', 'gy'), may hold values from 0 to 127, as said below
Outputs:
- head_new: float32 [80, 64, 512], P('scen', 'gx', 'gy'), parts along dimension 0
- boundary: float32 [128, 512], P(('scen', 'gx'), 'gy'), parts along dimension 0
- lake_new: float32 [128], P('scen'), parts along dimension 0
The draws below stay inside these ranges and needn't reach their ends.
There are 2 independent parts, one for each index of `scen`. The reference program is written for one: setup_inputs(seed, part) draws one part's arguments, and reference() takes and returns one part's arrays. A program takes and returns all parts, laid end to end along the dimension named above; an argument that names none is the same for every part. Nothing has to cross between parts.
Inputs may be any that keep to these rules, and one draw needn't show every extreme that they name: `pit_id`: values under 64 name a pit; larger values mark columns without a pit; a pit may own no column.
All inputs are finite; a program needn't handle non-finite values.
Results may differ from the reference program's by a relative error of at most 0.0001.
Values sent between devices are 32-bit elements; how exact they have to be, the bound alone decides.
A program may use at most 64 MiB of HBM per device.

```python
import math
import jax
import jax.numpy as jnp

LZ = 40
ITERS = 2
NPIT = 64
NCLASS = 12
NX = 64
NY = 512


def draw_pit_id(key, part):
    first, second = jax.random.split(key)
    third = jax.random.fold_in(key, 7)
    drawn_ids = jax.random.randint(first, (NX, NY), 0, 2 * NPIT, dtype=jnp.int32)
    shuffled = (jax.random.permutation(second, NPIT - 1) + 1).astype(jnp.int32)
    how_many = jax.random.randint(third, (), 2, 6, dtype=jnp.int32)
    chosen = (jnp.arange(NPIT - 1, dtype=jnp.int32) < how_many).astype(jnp.int32)
    table = jnp.zeros((2 * NPIT,), jnp.int32).at[shuffled].set(chosen)
    unused = table[drawn_ids] == 1
    return jnp.where(unused, drawn_ids + NPIT, drawn_ids).astype(jnp.int32)


def with_ends(values, stream_key, least, largest):
    spot = [jax.random.randint(jax.random.fold_in(stream_key, axis), (), 0, length) for axis, length in enumerate(values.shape)]
    longest = values.shape.index(max(values.shape))
    next_to = spot[:longest] + [(spot[longest] + 1) % values.shape[longest]] + spot[longest + 1:]
    return values.at[tuple(spot)].set(least).at[tuple(next_to)].set(largest)


def block_scale(stream_key, shape, cuts, least, top_value):
    def one(dim, blocks):
        heights = jax.random.uniform(jax.random.fold_in(jax.random.fold_in(stream_key, 6), dim), (blocks,), jnp.float32, least / len(cuts), top_value / len(cuts))
        return jnp.repeat(jnp.exp(heights), shape[dim] // blocks).reshape((-1,) + (1,) * (len(shape) - dim - 1))

    level = one(*cuts[0])
    for cut in cuts[1:]:
        level = level * one(*cut)
    return level


def setup_inputs(seed: int = 0, part: int = 0) -> dict:
    keys = jax.random.split(jax.random.key(seed), 9)
    own_keys = jax.random.split(jax.random.fold_in(keys[8], part), 9)
    head_old = jnp.clip(-3.0 + 4.0 * jax.random.uniform(own_keys[0], (LZ, NX, NY), jnp.float32) ** block_scale(own_keys[0], (LZ, NX, NY), ((1, 4), (2, 4)), -0.2, 0.2), -3.0, 1.0)
    soil_class = with_ends(jax.random.randint(keys[1], (LZ, NX, NY), 0, NCLASS), jax.random.fold_in(keys[1], 1), 0, NCLASS - 1).astype(jnp.int32)
    ksat_table = jnp.clip(jnp.exp(jax.random.uniform(keys[2], (NCLASS,), jnp.float32, math.log(0.05), math.log(2.0))), 0.05, 2.0)
    alpha_table = jnp.clip(jnp.exp(jax.random.uniform(keys[3], (NCLASS,), jnp.float32, math.log(0.3), math.log(2.0))), 0.3, 2.0)
    capacity_table = jnp.clip(jnp.exp(jax.random.uniform(keys[4], (NCLASS,), jnp.float32, math.log(0.2), math.log(2.0))), 0.2, 2.0)
    rain = jnp.clip(jnp.exp(math.log(2.0) - 2.9957323 * jax.random.uniform(own_keys[5], (NX, NY), jnp.float32) ** block_scale(own_keys[5], (NX, NY), ((0, 4), (1, 4)), -0.2, 0.2)), 0.1, 2.0)
    lake_level = jnp.clip(jax.random.uniform(own_keys[6], (NPIT,), jnp.float32, 0.0, 2.0), 0.0, 2.0)
    pit_id = draw_pit_id(jax.random.fold_in(keys[8], 71), part)
    return dict(head_old=head_old, soil_class=soil_class, ksat_table=ksat_table, alpha_table=alpha_table, capacity_table=capacity_table, rain=rain, lake_level=lake_level, pit_id=pit_id)


LEAK = 0.5
VERT = 2.0


def harmonic(first, second):
    return 2.0 * first * second / (first + second)


def reference(head_old, soil_class, ksat_table, alpha_table, capacity_table, rain, lake_level, pit_id):
    relative = jnp.exp(alpha_table[soil_class] * jnp.minimum(head_old, 0.0))
    cond = ksat_table[soil_class] * relative
    store = capacity_table[soil_class] * relative
    inpit = pit_id < NPIT
    safe_id = jnp.where(inpit, pit_id, 0)
    lake_cell = jnp.where(inpit, lake_level[safe_id], jnp.float32(0.0))
    leak_top = jnp.where(inpit, jnp.float32(LEAK), jnp.float32(0.0))
    extra = jnp.zeros_like(head_old).at[0].set(leak_top)
    tx = harmonic(cond[:, :-1, :], cond[:, 1:, :])
    ty = harmonic(cond[:, :, :-1], cond[:, :, 1:])
    tz = VERT * harmonic(cond[:-1], cond[1:])
    diag = store + extra
    diag = diag + jnp.pad(tx, ((0, 0), (1, 0), (0, 0))) + jnp.pad(tx, ((0, 0), (0, 1), (0, 0)))
    diag = diag + jnp.pad(ty, ((0, 0), (0, 0), (1, 0))) + jnp.pad(ty, ((0, 0), (0, 0), (0, 1)))
    diag = diag + jnp.pad(tz, ((1, 0), (0, 0), (0, 0))) + jnp.pad(tz, ((0, 1), (0, 0), (0, 0)))

    def operate(field):
        fx = tx * (field[:, 1:, :] - field[:, :-1, :])
        fy = ty * (field[:, :, 1:] - field[:, :, :-1])
        fz = tz * (field[1:] - field[:-1])
        out = (store + extra) * field
        out = out + jnp.pad(fx, ((0, 0), (1, 0), (0, 0))) - jnp.pad(fx, ((0, 0), (0, 1), (0, 0)))
        out = out + jnp.pad(fy, ((0, 0), (0, 0), (1, 0))) - jnp.pad(fy, ((0, 0), (0, 0), (0, 1)))
        out = out + jnp.pad(fz, ((1, 0), (0, 0), (0, 0))) - jnp.pad(fz, ((0, 1), (0, 0), (0, 0)))
        return out

    rhs = (store * head_old).at[0].add(rain + LEAK * lake_cell)
    solution = head_old
    residual = rhs - operate(head_old)
    precond = residual / diag
    direction = precond
    norm_now = jnp.sum(residual * precond)
    for step in range(ITERS):
        image = operate(direction)
        alpha = norm_now / jnp.sum(direction * image)
        solution = solution + alpha * direction
        residual = residual - alpha * image
        if step + 1 < ITERS:
            precond = residual / diag
            norm_next = jnp.sum(residual * precond)
            direction = precond + (norm_next / norm_now) * direction
            norm_now = norm_next
    top = solution[0]
    seep = jnp.where(inpit, LEAK * (lake_cell - top), jnp.float32(0.0))
    onehot = (pit_id[None, :, :] == jnp.arange(NPIT, dtype=jnp.int32)[:, None, None]).astype(jnp.float32)
    outflow = jnp.sum(onehot * seep[None], axis=(1, 2))
    inflow = jnp.sum(onehot * rain[None], axis=(1, 2))
    area = jnp.sum(onehot, axis=(1, 2))
    lake_new = lake_level + (inflow - outflow) / jnp.maximum(area, 1.0)
    boundary = jnp.where(inpit, lake_new[safe_id], top)
    return solution, boundary, lake_new
```

```python
import functools

import jax
import jax.numpy as jnp
from jax import lax
from jax.experimental import pallas as pl
from jax.experimental.pallas import tpu as pltpu
from jax.sharding import PartitionSpec as P

NPIT = 64
LEAK = 0.5
VERT = 2.0
CH = 4
MESH = pl.DeviceIdType.MESH
HIGH = lax.Precision.HIGHEST


def harmonic(first, second):
    return 2.0 * first * second / (first + second)


def kernel(
    nx, ny, lz, rows,
    head_hbm, soil_hbm, ksat_ref, alpha_ref, cap_ref, rain_ref, lake_ref, pit_ref,
    out_hbm, bnd_ref, lake_out_ref,
    H, SC, C, DG, TX, TY, TZ, R, Z, NZ, U, M,
    xs1, xr1, ys1, yr1, xs2, xr2, ys2, yr2, xs3, xr3, ys3, yr3,
    gather,
    local_sem, send_sem, recv_sem, ar_send, ar_recv,
):
    f32 = jnp.float32
    mx, my = lax.axis_index("gx"), lax.axis_index("gy")
    n = nx * ny
    me = mx * ny + my
    cells = lz * rows
    lo_pad = rows
    step_rows = CH * rows
    steps = lz // CH

    in_h = pltpu.make_async_copy(head_hbm, H.at[pl.ds(lo_pad, cells)], local_sem.at[0])
    in_s = pltpu.make_async_copy(soil_hbm, SC, local_sem.at[1])
    in_h.start()
    in_s.start()

    def peer(s):
        other = lax.rem(me + s, n)
        return {"gx": lax.div(other, ny), "gy": lax.rem(other, ny)}

    def each_peer(body):
        if n <= 16:
            for s in range(1, n):
                body(s)
        else:
            lax.fori_loop(1, n, lambda s, c: (body(s), c)[1], 0)

    barrier = pltpu.get_barrier_semaphore()
    each_peer(lambda s: pl.semaphore_signal(barrier, inc=1, device_id=peer(s), device_id_type=MESH))

    has = {("x", 0): mx > 0, ("x", 1): mx < nx - 1, ("y", 0): my > 0, ("y", 1): my < ny - 1}
    dev = {
        ("x", 0): {"gx": jnp.maximum(mx - 1, 0)},
        ("x", 1): {"gx": jnp.minimum(mx + 1, nx - 1)},
        ("y", 0): {"gy": jnp.maximum(my - 1, 0)},
        ("y", 1): {"gy": jnp.minimum(my + 1, ny - 1)},
    }

    def copy(ax, side, src, dst, number):
        return pltpu.make_async_remote_copy(
            src_ref=src.at[side], dst_ref=dst.at[1 - side],
            send_sem=send_sem.at[number + side], recv_sem=recv_sem.at[number + 1 - side],
            device_id=dev[ax, side], device_id_type=MESH,
        )

    def send(ax, src, dst, number, sides=(0, 1)):
        for side in sides:
            @pl.when(has[ax, side])
            def _(side=side):
                copy(ax, side, src, dst, number).start()

    def receive(ax, src, dst, number, sides=(0, 1)):
        for side in sides:
            @pl.when(has[ax, side])
            def _(side=side):
                copy(ax, 1 - side, src, dst, number).wait_recv()

    def sent(ax, src, dst, number, sides=(0, 1)):
        for side in sides:
            @pl.when(has[ax, side])
            def _(side=side):
                copy(ax, side, src, dst, number).wait_send()

    for ax, buf in (("x", xr1), ("y", yr1), ("x", xr2), ("y", yr2)):
        for side in (0, 1):
            @pl.when(jnp.logical_not(has[ax, side]))
            def _(buf=buf, side=side):
                buf[side] = jnp.zeros(buf.shape[1:], f32)
    for ax, buf in (("x", xr3), ("y", yr3)):
        @pl.when(jnp.logical_not(has[ax, 1]))
        def _(buf=buf):
            buf[1] = jnp.zeros(buf.shape[1:], f32)

    for ref in (H, C, Z, U):
        ref[pl.ds(0, rows), :] = jnp.zeros((rows, 128), f32)
        ref[pl.ds(lo_pad + cells, rows), :] = jnp.zeros((rows, 128), f32)
    TZ[pl.ds(0, rows), :] = jnp.zeros((rows, 128), f32)

    pit = pit_ref[...]
    for i in range(rows):
        ids = lax.broadcasted_iota(jnp.int32, (128, 128), 0)
        M[:, i * 128:(i + 1) * 128] = jnp.where(ids == pit[i:i + 1, :], f32(1), f32(0))

    def spread(row):
        flat = jnp.dot(jnp.broadcast_to(row, (8, 128)), M[...], precision=HIGH, preferred_element_type=f32)
        return jnp.concatenate([flat[0:1, i * 128:(i + 1) * 128] for i in range(rows)], axis=0)

    def flatten(field):
        return jnp.concatenate([field[i:i + 1, :] for i in range(rows)], axis=1)

    def by_pit(flat):
        return lax.dot_general(flat, M[...], (((1,), (1,)), ((), ())), precision=HIGH, preferred_element_type=f32)

    def at(k, shift=0):
        return pl.ds(pl.multiple_of(lo_pad + k * step_rows + shift * rows, rows), step_rows)

    def at0(k):
        return pl.ds(pl.multiple_of(k * step_rows, rows), step_rows)

    in_h.wait()
    in_s.wait()

    @pl.loop(0, steps)
    def _(k):
        classes = SC[at0(k), :]
        ks = jnp.zeros(classes.shape, f32)
        al = jnp.zeros(classes.shape, f32)
        cp = jnp.zeros(classes.shape, f32)
        for which in range(ksat_ref.shape[0]):
            match = classes == which
            ks = jnp.where(match, ksat_ref[which], ks)
            al = jnp.where(match, alpha_ref[which], al)
            cp = jnp.where(match, cap_ref[which], cp)
        relative = jnp.exp(al * jnp.minimum(H[at(k), :], 0.0))
        C[at(k), :] = ks * relative
        DG[at0(k), :] = cp * relative

    def edge(ref, which, pad):
        return ref[pl.ds(pad + which, lz, stride=rows), :]

    c_first, c_last = edge(C, 0, lo_pad), edge(C, rows - 1, lo_pad)
    h_first, h_last = edge(H, 0, lo_pad), edge(H, rows - 1, lo_pad)
    xs1[0, 0], xs1[0, 1] = c_first, h_first
    xs1[1, 0], xs1[1, 1] = c_last, h_last

    def columns(ref, pad):
        turned = ref[pl.ds(pad, cells), :].T
        return turned[0:1, :], turned[127:128, :]

    def to_block(low, high):
        r = lax.broadcasted_iota(jnp.int32, (8, cells), 0)
        top = jnp.where(r == 0, low, f32(0))
        bottom = jnp.where(r == 7, high, f32(0))
        return jnp.concatenate([top, jnp.zeros((112, cells), f32), bottom], axis=0).T

    pl.semaphore_wait(barrier, n - 1)
    send("x", xs1, xr1, 0)
    cy = columns(C, lo_pad)
    hy = columns(H, lo_pad)
    for side in (0, 1):
        ys1[side, 0:1, :] = cy[side]
        ys1[side, 1:2, :] = hy[side]
    send("y", ys1, yr1, 2)

    shape3 = (CH, rows, 128)
    lane = lax.broadcasted_iota(jnp.int32, shape3, 2)
    sub = lax.broadcasted_iota(jnp.int32, shape3, 1)

    def rx(v, s):
        return pltpu.roll(v, s % rows, 1)

    def ry(v, s):
        return pltpu.roll(v, s % 128, 2)

    def get(ref, k, shift=0):
        return ref[at(k, shift), :].reshape(shape3)

    def get0(ref, k):
        return ref[at0(k), :].reshape(shape3)

    def put0(ref, k, v):
        ref[at0(k), :] = v.reshape(step_rows, 128)

    def put(ref, k, v):
        ref[at(k), :] = v.reshape(step_rows, 128)

    @pl.loop(0, steps)
    def _(k):
        c, h = get(C, k), get(H, k)
        tx = jnp.where(sub == rows - 1, 0.0, harmonic(c, rx(c, -1)))
        ty = jnp.where(lane == 127, 0.0, harmonic(c, ry(c, -1)))
        tz = VERT * harmonic(c, get(C, k, 1))
        put0(TX, k, tx)
        put0(TY, k, ty)
        put(TZ, k, tz)
        fx = tx * (rx(h, -1) - h)
        fy = ty * (ry(h, -1) - h)
        fz = tz * (get(H, k, 1) - h)
        tz_low = get(TZ, k, -1)
        fz_low = tz_low * (h - get(H, k, -1))
        put0(DG, k, get0(DG, k) + tx + rx(tx, 1) + ty + ry(ty, 1) + tz + tz_low)
        put0(R, k, fx - rx(fx, 1) + fy - ry(fy, 1) + fz - fz_low)

    inpit = pit < NPIT
    lake_row = lake_ref[...]
    lake_wide = jnp.concatenate([lake_row, jnp.zeros((1, 128 - NPIT), f32)], axis=1)
    lake_cell = spread(lake_wide)
    top_h = H[pl.ds(lo_pad, rows), :]
    rain = rain_ref[...]
    top_rows = pl.ds(0, rows)
    DG[top_rows, :] += jnp.where(inpit, f32(LEAK), f32(0))
    R[top_rows, :] += rain + jnp.where(inpit, LEAK * (lake_cell - top_h), f32(0))
    r8 = lax.broadcasted_iota(jnp.int32, (8, rows * 128), 0)
    early = by_pit(jnp.where(r8 == 0, flatten(rain), jnp.where(r8 == 1, f32(1), flatten(top_h))))

    receive("x", xs1, xr1, 0)
    tx_low = harmonic(c_first, xr1[0, 0])
    tx_high = harmonic(c_last, xr1[1, 0])
    first = pl.ds(0, lz, stride=rows)
    last = pl.ds(rows - 1, lz, stride=rows)
    DG[first, :] += tx_low
    DG[last, :] += tx_high
    R[first, :] += tx_low * (xr1[0, 1] - h_first)
    R[last, :] += tx_high * (xr1[1, 1] - h_last)
    receive("y", ys1, yr1, 2)
    ty_low = harmonic(cy[0], yr1[0, 0:1, :])
    ty_high = harmonic(cy[1], yr1[1, 0:1, :])
    NZ[...] = to_block(ty_low, ty_high)
    U[pl.ds(lo_pad, cells), :] = to_block(
        ty_low * (yr1[0, 1:2, :] - hy[0]), ty_high * (yr1[1, 1:2, :] - hy[1])
    )

    zero_acc = jnp.zeros(shape3, f32)

    def make_z(k, acc):
        inverse = 1.0 / (get0(DG, k) + get0(NZ, k))
        r = get0(R, k) + get(U, k)
        z = r * inverse
        put0(DG, k, inverse)
        put0(R, k, r)
        put(Z, k, z)
        return acc + r * z

    acc_a = lax.fori_loop(0, steps, make_z, zero_acc)

    xs2[0] = edge(Z, 0, lo_pad)
    xs2[1] = edge(Z, rows - 1, lo_pad)
    send("x", xs2, xr2, 4)
    zy = columns(Z, lo_pad)
    for side in (0, 1):
        ys2[side] = zy[side]
    send("y", ys2, yr2, 6)

    @pl.loop(0, steps)
    def _(k):
        z, tx, ty = get(Z, k), get0(TX, k), get0(TY, k)
        out = tx * rx(z, -1) + rx(tx * z, 1)
        out = out + ty * ry(z, -1) + ry(ty * z, 1)
        put0(NZ, k, out + get(TZ, k) * get(Z, k, 1) + get(TZ, k, -1) * get(Z, k, -1))

    ones8 = jnp.zeros((8, rows * 128), f32)
    mid = by_pit(flatten(Z[pl.ds(lo_pad, rows), :]) + ones8)

    receive("x", xs2, xr2, 4)
    NZ[first, :] += tx_low * xr2[0]
    NZ[last, :] += tx_high * xr2[1]
    receive("y", ys2, yr2, 6)
    U[pl.ds(lo_pad, cells), :] = to_block(ty_low * yr2[0], ty_high * yr2[1])

    def make_u(k, acc):
        nz = get0(NZ, k) + get(U, k)
        u = nz * get0(DG, k)
        put(U, k, u)
        return acc[0] + get0(R, k) * u, acc[1] + nz * u

    acc_g, acc_c = lax.fori_loop(0, steps, make_u, (zero_acc, zero_acc))

    xs3[0] = edge(U, 0, lo_pad)
    send("x", xs3, xr3, 8, (0,))
    uy = columns(U, lo_pad)
    ys3[0] = uy[0]
    send("y", ys3, yr3, 10, (0,))

    def make_f(k, acc):
        u = get(U, k)
        inner = get0(TX, k) * rx(u, -1) + get0(TY, k) * ry(u, -1) + get(TZ, k) * get(U, k, 1)
        return acc + u * inner

    acc_f = lax.fori_loop(0, steps, make_f, zero_acc)
    late = by_pit(flatten(U[pl.ds(lo_pad, rows), :]) + ones8)

    def row_sum(acc):
        return jnp.sum(jnp.sum(acc, axis=0), axis=0, keepdims=True)

    sum_a, sum_g, sum_c, sum_f = row_sum(acc_a), row_sum(acc_g), row_sum(acc_c), row_sum(acc_f)
    u_last = edge(U, rows - 1, lo_pad)
    receive("x", xs3, xr3, 8, (1,))
    sum_f = sum_f + jnp.sum(u_last * tx_high * xr3[1], axis=0, keepdims=True)
    receive("y", ys3, yr3, 10, (1,))
    cross = uy[1] * ty_high * yr3[1]
    for i in range(cells // 128):
        sum_f = sum_f + cross[:, i * 128:(i + 1) * 128]
    sum_f = 2.0 * sum_f

    r1 = lax.broadcasted_iota(jnp.int32, (8, 128), 0)
    l1 = lax.broadcasted_iota(jnp.int32, (8, 128), 1)
    scal = jnp.where(r1 == 0, sum_a, jnp.where(r1 == 1, sum_g, jnp.where(r1 == 2, sum_c, sum_f)))
    scal = scal + pltpu.roll(scal, 64, 1)
    pits = jnp.where(r1 < 3, early, jnp.where(r1 == 3, mid, late))
    gather[me] = jnp.where(l1 < NPIT, pits, scal)

    def reduce_copy(s):
        return pltpu.make_async_remote_copy(
            src_ref=gather.at[me], dst_ref=gather.at[me], send_sem=ar_send.at[s], recv_sem=ar_recv.at[me],
            device_id=peer(s), device_id_type=MESH,
        )

    def arrival(s):
        source = lax.rem(me + s, n)
        return pltpu.make_async_remote_copy(
            src_ref=gather.at[source], dst_ref=gather.at[source], send_sem=ar_send.at[s], recv_sem=ar_recv.at[source],
            device_id=peer(s), device_id_type=MESH,
        )

    each_peer(lambda s: reduce_copy(s).start())
    each_peer(lambda s: arrival(s).wait_recv())
    if n <= 16:
        total = gather[0]
        for j in range(1, n):
            total = total + gather[j]
    else:
        total = lax.fori_loop(1, n, lambda j, t: t + gather[j], gather[0])

    scalars = jnp.sum(jnp.where(l1 < NPIT, f32(0), total), axis=1, keepdims=True)
    a, g, c, f = (scalars[i:i + 1, :] for i in range(4))
    b = a - g
    step0 = a / b
    ratio = (a * c - g * g) / (b * b)
    p = ratio - g / b
    step1 = a * ratio / (p * p * b + 2.0 * p * step0 * (g - c) + step0 * step0 * (c - f))
    coef_z = step0 + step1 * p
    coef_u = step1 * step0

    coef_z3, coef_u3 = coef_z.reshape(1, 1, 1), coef_u.reshape(1, 1, 1)

    @pl.loop(0, steps)
    def _(k):
        put0(NZ, k, get(H, k) + coef_z3 * get(Z, k) + coef_u3 * get(U, k))

    out_copy = pltpu.make_async_copy(NZ, out_hbm, local_sem.at[0])
    out_copy.start()

    inflow, area = total[0:1, :NPIT], total[1:2, :NPIT]
    top_sum = total[2:3, :NPIT] + coef_z * total[3:4, :NPIT] + coef_u * total[4:5, :NPIT]
    outflow = LEAK * (lake_row * area - top_sum)
    lake_new = lake_row + (inflow - outflow) / jnp.maximum(area, 1.0)
    lake_out_ref[...] = lake_new
    lake_new_cell = spread(jnp.concatenate([lake_new, jnp.zeros((1, 128 - NPIT), f32)], axis=1))
    bnd_ref[...] = jnp.where(inpit, lake_new_cell, NZ[pl.ds(0, rows), :])

    sent("x", xs1, xr1, 0)
    sent("y", ys1, yr1, 2)
    sent("x", xs2, xr2, 4)
    sent("y", ys2, yr2, 6)
    sent("x", xs3, xr3, 8, (0,))
    sent("y", ys3, yr3, 10, (0,))
    each_peer(lambda s: reduce_copy(s).wait_send())
    out_copy.wait()


def solution(mesh):
    nx, ny = mesh.shape["gx"], mesh.shape["gy"]

    def shards(head_old, soil_class, ksat_table, alpha_table, capacity_table, rain, lake_level, pit_id):
        lz, rows, width = head_old.shape
        cells = lz * rows
        f32 = jnp.float32
        block = pltpu.VMEM((cells, width), f32)
        padded = pltpu.VMEM((cells + 2 * rows, width), f32)
        vmem = pl.BlockSpec(memory_space=pltpu.VMEM)
        smem = pl.BlockSpec(memory_space=pltpu.SMEM)
        hbm = pl.BlockSpec(memory_space=pl.ANY)
        n = nx * ny
        out, boundary, lake_new = pl.pallas_call(
            functools.partial(kernel, nx, ny, lz, rows),
            out_shape=(
                jax.ShapeDtypeStruct((cells, width), f32),
                jax.ShapeDtypeStruct((rows, width), f32),
                jax.ShapeDtypeStruct((1, NPIT), f32),
            ),
            in_specs=[hbm, hbm, smem, smem, smem, vmem, vmem, vmem],
            out_specs=(hbm, vmem, vmem),
            scratch_shapes=[
                padded, pltpu.VMEM((cells, width), jnp.int32), padded, block, block, block, padded,
                block, padded, block, padded, pltpu.VMEM((128, rows * 128), f32),
                pltpu.VMEM((2, 2, lz, width), f32), pltpu.VMEM((2, 2, lz, width), f32),
                pltpu.VMEM((2, 2, cells), f32), pltpu.VMEM((2, 2, cells), f32),
                pltpu.VMEM((2, lz, width), f32), pltpu.VMEM((2, lz, width), f32),
                pltpu.VMEM((2, 1, cells), f32), pltpu.VMEM((2, 1, cells), f32),
                pltpu.VMEM((2, lz, width), f32), pltpu.VMEM((2, lz, width), f32),
                pltpu.VMEM((2, 1, cells), f32), pltpu.VMEM((2, 1, cells), f32),
                pltpu.VMEM((n, 8, 128), f32),
                pltpu.SemaphoreType.DMA((2,)),
                pltpu.SemaphoreType.DMA((12,)), pltpu.SemaphoreType.DMA((12,)),
                pltpu.SemaphoreType.DMA((n,)), pltpu.SemaphoreType.DMA((n,)),
            ],
            compiler_params=pltpu.CompilerParams(
                collective_id=0, has_side_effects=True, vmem_limit_bytes=40 * 1024 * 1024
            ),
            name="step",
        )(
            head_old.reshape(cells, width), soil_class.reshape(cells, width),
            ksat_table, alpha_table, capacity_table, rain, lake_level.reshape(1, NPIT), pit_id,
        )
        return out.reshape(lz, rows, width), boundary, lake_new.reshape(NPIT)

    return jax.shard_map(
        shards,
        mesh=mesh,
        in_specs=(
            P("scen", "gx", "gy"),
            P(None, "gx", "gy"),
            P(),
            P(),
            P(),
            P(("scen", "gx"), "gy"),
            P("scen"),
            P("gx", "gy"),
        ),
        out_specs=(P("scen", "gx", "gy"), P(("scen", "gx"), "gy"), P("scen")),
        check_vma=False,
    )
```

```python
import functools

import jax
import jax.numpy as jnp
from jax import lax
from jax.experimental import pallas as pl
from jax.experimental.pallas import tpu as pltpu
from jax.sharding import PartitionSpec as P

NPIT = 64
LEAK = 0.5
VERT = 2.0
CH = 20
MESH = pl.DeviceIdType.MESH
HIGH = lax.Precision.HIGHEST


def harmonic(first, second):
    return 2.0 * first * second / (first + second)


def kernel(
    nx, ny, lz, rows,
    head_hbm, soil_hbm, ksat_hbm, alpha_hbm, cap_hbm, rain_hbm, lake_hbm, pit_hbm,
    out_ref, bnd_ref, lake_out_ref,
    ksat_ref, alpha_ref, cap_ref, rain_ref, lake_ref, pit_ref, H, SC, C, DG, TX, TY, TZ, R, Z, NZ, U, M,
    xs1, xr1, ys1, yr1, xs2, xr2, ys2, yr2, xs3, xr3, ys3, yr3,
    gather,
    local_sem, send_sem, recv_sem, ar_send, ar_recv,
):
    f32 = jnp.float32
    mx, my = lax.axis_index("gx"), lax.axis_index("gy")
    n = nx * ny
    me = mx * ny + my
    cells = lz * rows
    lo_pad = rows
    step_rows = CH * rows
    steps = lz // CH

    in_h = pltpu.make_async_copy(head_hbm, H.at[pl.ds(lo_pad, cells)], local_sem.at[0])
    in_s = pltpu.make_async_copy(soil_hbm, SC, local_sem.at[1])
    small = [
        pltpu.make_async_copy(src, dst, local_sem.at[2 + i])
        for i, (src, dst) in enumerate((
            (ksat_hbm, ksat_ref), (alpha_hbm, alpha_ref), (cap_hbm, cap_ref),
            (rain_hbm, rain_ref), (lake_hbm, lake_ref), (pit_hbm, pit_ref),
        ))
    ]
    for each in small[:3] + [in_s, in_h] + small[3:]:
        each.start()

    def peer(s):
        other = lax.rem(me + s, n)
        return {"gx": lax.div(other, ny), "gy": lax.rem(other, ny)}

    def each_peer(body):
        if n <= 16:
            for s in range(1, n):
                body(s)
        else:
            lax.fori_loop(1, n, lambda s, c: (body(s), c)[1], 0)

    barrier = pltpu.get_barrier_semaphore()
    each_peer(lambda s: pl.semaphore_signal(barrier, inc=1, device_id=peer(s), device_id_type=MESH))

    has = {("x", 0): mx > 0, ("x", 1): mx < nx - 1, ("y", 0): my > 0, ("y", 1): my < ny - 1}
    dev = {
        ("x", 0): {"gx": jnp.maximum(mx - 1, 0)},
        ("x", 1): {"gx": jnp.minimum(mx + 1, nx - 1)},
        ("y", 0): {"gy": jnp.maximum(my - 1, 0)},
        ("y", 1): {"gy": jnp.minimum(my + 1, ny - 1)},
    }

    def copy(ax, side, src, dst, number):
        return pltpu.make_async_remote_copy(
            src_ref=src.at[side], dst_ref=dst.at[1 - side],
            send_sem=send_sem.at[number + side], recv_sem=recv_sem.at[number + 1 - side],
            device_id=dev[ax, side], device_id_type=MESH,
        )

    def send(ax, src, dst, number, sides=(0, 1)):
        for side in sides:
            @pl.when(has[ax, side])
            def _(side=side):
                copy(ax, side, src, dst, number).start()

    def receive(ax, src, dst, number, sides=(0, 1)):
        for side in sides:
            @pl.when(has[ax, side])
            def _(side=side):
                copy(ax, 1 - side, src, dst, number).wait_recv()

    def sent(ax, src, dst, number, sides=(0, 1)):
        for side in sides:
            @pl.when(has[ax, side])
            def _(side=side):
                copy(ax, side, src, dst, number).wait_send()

    for ax, buf in (("x", xr1), ("y", yr1), ("x", xr2), ("y", yr2)):
        for side in (0, 1):
            @pl.when(jnp.logical_not(has[ax, side]))
            def _(buf=buf, side=side):
                buf[side] = jnp.zeros(buf.shape[1:], f32)
    for ax, buf in (("x", xr3), ("y", yr3)):
        @pl.when(jnp.logical_not(has[ax, 1]))
        def _(buf=buf):
            buf[1] = jnp.zeros(buf.shape[1:], f32)

    for ref in (H, C, Z, U):
        ref[pl.ds(0, rows), :] = jnp.zeros((rows, 128), f32)
        ref[pl.ds(lo_pad + cells, rows), :] = jnp.zeros((rows, 128), f32)
    TZ[pl.ds(0, rows), :] = jnp.zeros((rows, 128), f32)

    def spread(row):
        flat = jnp.dot(jnp.broadcast_to(row, (8, 128)), M[...], precision=HIGH, preferred_element_type=f32)
        return jnp.concatenate([flat[0:1, i * 128:(i + 1) * 128] for i in range(rows)], axis=0)

    def flatten(field):
        return jnp.concatenate([field[i:i + 1, :] for i in range(rows)], axis=1)

    def by_pit(flat):
        return lax.dot_general(flat, M[...], (((1,), (1,)), ((), ())), precision=HIGH, preferred_element_type=f32)

    def at(k, shift=0):
        return pl.ds(pl.multiple_of(lo_pad + k * step_rows + shift * rows, rows), step_rows)

    def at0(k):
        return pl.ds(pl.multiple_of(k * step_rows, rows), step_rows)

    for each in small[:3]:
        each.wait()
    in_s.wait()
    in_h.wait()

    @pl.loop(0, steps)
    def _(k):
        classes = SC[at0(k), :]
        ks = jnp.zeros(classes.shape, f32)
        al = jnp.zeros(classes.shape, f32)
        cp = jnp.zeros(classes.shape, f32)
        for which in range(ksat_ref.shape[0]):
            match = classes == which
            ks = jnp.where(match, ksat_ref[which], ks)
            al = jnp.where(match, alpha_ref[which], al)
            cp = jnp.where(match, cap_ref[which], cp)
        relative = jnp.exp(al * jnp.minimum(H[at(k), :], 0.0))
        C[at(k), :] = ks * relative
        DG[at0(k), :] = cp * relative

    def edge(ref, which, pad):
        return ref[pl.ds(pad + which, lz, stride=rows), :]

    c_first, c_last = edge(C, 0, lo_pad), edge(C, rows - 1, lo_pad)
    h_first, h_last = edge(H, 0, lo_pad), edge(H, rows - 1, lo_pad)
    xs1[0, 0], xs1[0, 1] = c_first, h_first
    xs1[1, 0], xs1[1, 1] = c_last, h_last

    def columns(ref, pad):
        turned = ref[pl.ds(pad, cells), :].T
        return turned[0:1, :], turned[127:128, :]

    def to_block(low, high):
        r = lax.broadcasted_iota(jnp.int32, (8, cells), 0)
        top = jnp.where(r == 0, low, f32(0))
        bottom = jnp.where(r == 7, high, f32(0))
        return jnp.concatenate([top, jnp.zeros((112, cells), f32), bottom], axis=0).T

    pl.semaphore_wait(barrier, n - 1)
    send("x", xs1, xr1, 0)
    cy = columns(C, lo_pad)
    hy = columns(H, lo_pad)
    for side in (0, 1):
        ys1[side, 0:1, :] = cy[side]
        ys1[side, 1:2, :] = hy[side]
    send("y", ys1, yr1, 2)

    shape3 = (CH, rows, 128)
    lane = lax.broadcasted_iota(jnp.int32, shape3, 2)
    sub = lax.broadcasted_iota(jnp.int32, shape3, 1)

    def rx(v, s):
        return pltpu.roll(v, s % rows, 1)

    def ry(v, s):
        return pltpu.roll(v, s % 128, 2)

    def get(ref, k, shift=0):
        return ref[at(k, shift), :].reshape(shape3)

    def get0(ref, k):
        return ref[at0(k), :].reshape(shape3)

    def put0(ref, k, v):
        ref[at0(k), :] = v.reshape(step_rows, 128)

    def put(ref, k, v):
        ref[at(k), :] = v.reshape(step_rows, 128)

    @pl.loop(0, steps)
    def _(k):
        c, h = get(C, k), get(H, k)
        tx = jnp.where(sub == rows - 1, 0.0, harmonic(c, rx(c, -1)))
        ty = jnp.where(lane == 127, 0.0, harmonic(c, ry(c, -1)))
        tz = VERT * harmonic(c, get(C, k, 1))
        put0(TX, k, tx)
        put0(TY, k, ty)
        put(TZ, k, tz)
        fx = tx * (rx(h, -1) - h)
        fy = ty * (ry(h, -1) - h)
        fz = tz * (get(H, k, 1) - h)
        tz_low = get(TZ, k, -1)
        fz_low = tz_low * (h - get(H, k, -1))
        put0(DG, k, get0(DG, k) + tx + rx(tx, 1) + ty + ry(ty, 1) + tz + tz_low)
        put0(R, k, fx - rx(fx, 1) + fy - ry(fy, 1) + fz - fz_low)

    for each in small[3:]:
        each.wait()
    pit = pit_ref[...]
    for i in range(rows):
        ids = lax.broadcasted_iota(jnp.int32, (128, 128), 0)
        M[:, i * 128:(i + 1) * 128] = jnp.where(ids == pit[i:i + 1, :], f32(1), f32(0))

    inpit = pit < NPIT
    lake_row = lake_ref[...]
    lake_wide = jnp.concatenate([lake_row, jnp.zeros((1, 128 - NPIT), f32)], axis=1)
    lake_cell = spread(lake_wide)
    top_h = H[pl.ds(lo_pad, rows), :]
    rain = rain_ref[...]
    top_rows = pl.ds(0, rows)
    DG[top_rows, :] += jnp.where(inpit, f32(LEAK), f32(0))
    R[top_rows, :] += rain + jnp.where(inpit, LEAK * (lake_cell - top_h), f32(0))
    r8 = lax.broadcasted_iota(jnp.int32, (8, rows * 128), 0)
    early = by_pit(jnp.where(r8 == 0, flatten(rain), jnp.where(r8 == 1, f32(1), flatten(top_h))))

    receive("x", xs1, xr1, 0)
    tx_low = harmonic(c_first, xr1[0, 0])
    tx_high = harmonic(c_last, xr1[1, 0])
    first = pl.ds(0, lz, stride=rows)
    last = pl.ds(rows - 1, lz, stride=rows)
    DG[first, :] += tx_low
    DG[last, :] += tx_high
    R[first, :] += tx_low * (xr1[0, 1] - h_first)
    R[last, :] += tx_high * (xr1[1, 1] - h_last)
    receive("y", ys1, yr1, 2)
    ty_low = harmonic(cy[0], yr1[0, 0:1, :])
    ty_high = harmonic(cy[1], yr1[1, 0:1, :])
    NZ[...] = to_block(ty_low, ty_high)
    U[pl.ds(lo_pad, cells), :] = to_block(
        ty_low * (yr1[0, 1:2, :] - hy[0]), ty_high * (yr1[1, 1:2, :] - hy[1])
    )

    zero_acc = jnp.zeros(shape3, f32)

    def make_z(k, acc):
        inverse = 1.0 / (get0(DG, k) + get0(NZ, k))
        r = get0(R, k) + get(U, k)
        z = r * inverse
        put0(DG, k, inverse)
        put0(R, k, r)
        put(Z, k, z)
        return acc + r * z

    acc_a = lax.fori_loop(0, steps, make_z, zero_acc)

    xs2[0] = edge(Z, 0, lo_pad)
    xs2[1] = edge(Z, rows - 1, lo_pad)
    send("x", xs2, xr2, 4)
    zy = columns(Z, lo_pad)
    for side in (0, 1):
        ys2[side] = zy[side]
    send("y", ys2, yr2, 6)

    @pl.loop(0, steps)
    def _(k):
        z, tx, ty = get(Z, k), get0(TX, k), get0(TY, k)
        out = tx * rx(z, -1) + rx(tx * z, 1)
        out = out + ty * ry(z, -1) + ry(ty * z, 1)
        put0(NZ, k, out + get(TZ, k) * get(Z, k, 1) + get(TZ, k, -1) * get(Z, k, -1))

    ones8 = jnp.zeros((8, rows * 128), f32)
    mid = by_pit(flatten(Z[pl.ds(lo_pad, rows), :]) + ones8)

    receive("x", xs2, xr2, 4)
    NZ[first, :] += tx_low * xr2[0]
    NZ[last, :] += tx_high * xr2[1]
    receive("y", ys2, yr2, 6)
    U[pl.ds(lo_pad, cells), :] = to_block(ty_low * yr2[0], ty_high * yr2[1])

    def make_u(k, acc):
        nz = get0(NZ, k) + get(U, k)
        u = nz * get0(DG, k)
        put(U, k, u)
        return acc[0] + get0(R, k) * u, acc[1] + nz * u

    acc_g, acc_c = lax.fori_loop(0, steps, make_u, (zero_acc, zero_acc))

    xs3[0] = edge(U, 0, lo_pad)
    send("x", xs3, xr3, 8, (0,))
    uy = columns(U, lo_pad)
    ys3[0] = uy[0]
    send("y", ys3, yr3, 10, (0,))

    def make_f(k, acc):
        u = get(U, k)
        inner = get0(TX, k) * rx(u, -1) + get0(TY, k) * ry(u, -1) + get(TZ, k) * get(U, k, 1)
        return acc + u * inner

    acc_f = lax.fori_loop(0, steps, make_f, zero_acc)
    late = by_pit(flatten(U[pl.ds(lo_pad, rows), :]) + ones8)

    def row_sum(acc):
        return jnp.sum(jnp.sum(acc, axis=0), axis=0, keepdims=True)

    sum_a, sum_g, sum_c, sum_f = row_sum(acc_a), row_sum(acc_g), row_sum(acc_c), row_sum(acc_f)
    u_last = edge(U, rows - 1, lo_pad)
    receive("x", xs3, xr3, 8, (1,))
    sum_f = sum_f + jnp.sum(u_last * tx_high * xr3[1], axis=0, keepdims=True)
    receive("y", ys3, yr3, 10, (1,))
    cross = uy[1] * ty_high * yr3[1]
    for i in range(cells // 128):
        sum_f = sum_f + cross[:, i * 128:(i + 1) * 128]
    sum_f = 2.0 * sum_f

    r1 = lax.broadcasted_iota(jnp.int32, (8, 128), 0)
    l1 = lax.broadcasted_iota(jnp.int32, (8, 128), 1)
    scal = jnp.where(r1 == 0, sum_a, jnp.where(r1 == 1, sum_g, jnp.where(r1 == 2, sum_c, sum_f)))
    scal = scal + pltpu.roll(scal, 64, 1)
    pits = jnp.where(r1 < 3, early, jnp.where(r1 == 3, mid, late))
    gather[me] = jnp.where(l1 < NPIT, pits, scal)

    def reduce_copy(s):
        return pltpu.make_async_remote_copy(
            src_ref=gather.at[me], dst_ref=gather.at[me], send_sem=ar_send.at[s], recv_sem=ar_recv.at[me],
            device_id=peer(s), device_id_type=MESH,
        )

    def arrival(s):
        source = lax.rem(me + s, n)
        return pltpu.make_async_remote_copy(
            src_ref=gather.at[source], dst_ref=gather.at[source], send_sem=ar_send.at[s], recv_sem=ar_recv.at[source],
            device_id=peer(s), device_id_type=MESH,
        )

    each_peer(lambda s: reduce_copy(s).start())
    each_peer(lambda s: arrival(s).wait_recv())
    if n <= 16:
        total = gather[0]
        for j in range(1, n):
            total = total + gather[j]
    else:
        total = lax.fori_loop(1, n, lambda j, t: t + gather[j], gather[0])

    scalars = jnp.sum(jnp.where(l1 < NPIT, f32(0), total), axis=1, keepdims=True)
    a, g, c, f = (scalars[i:i + 1, :] for i in range(4))
    b = a - g
    step0 = a / b
    ratio = (a * c - g * g) / (b * b)
    p = ratio - g / b
    step1 = a * ratio / (p * p * b + 2.0 * p * step0 * (g - c) + step0 * step0 * (c - f))
    coef_z = step0 + step1 * p
    coef_u = step1 * step0

    coef_z3, coef_u3 = coef_z.reshape(1, 1, 1), coef_u.reshape(1, 1, 1)

    @pl.loop(0, steps)
    def _(k):
        put0(out_ref, k, get(H, k) + coef_z3 * get(Z, k) + coef_u3 * get(U, k))

    inflow, area = total[0:1, :NPIT], total[1:2, :NPIT]
    top_sum = total[2:3, :NPIT] + coef_z * total[3:4, :NPIT] + coef_u * total[4:5, :NPIT]
    outflow = LEAK * (lake_row * area - top_sum)
    lake_new = lake_row + (inflow - outflow) / jnp.maximum(area, 1.0)
    lake_out_ref[...] = lake_new
    lake_new_cell = spread(jnp.concatenate([lake_new, jnp.zeros((1, 128 - NPIT), f32)], axis=1))
    bnd_ref[...] = jnp.where(inpit, lake_new_cell, out_ref[pl.ds(0, rows), :])

    sent("x", xs1, xr1, 0)
    sent("y", ys1, yr1, 2)
    sent("x", xs2, xr2, 4)
    sent("y", ys2, yr2, 6)
    sent("x", xs3, xr3, 8, (0,))
    sent("y", ys3, yr3, 10, (0,))
    each_peer(lambda s: reduce_copy(s).wait_send())


def write_out(a_ref, b_ref, c_ref, a_out, b_out, c_out, sems):
    pairs = ((a_ref, a_out), (b_ref, b_out), (c_ref, c_out))
    copies = [pltpu.make_async_copy(src, dst, sems.at[i]) for i, (src, dst) in enumerate(pairs)]
    for each in copies:
        each.start()
    for each in copies:
        each.wait()


def solution(mesh):
    nx, ny = mesh.shape["gx"], mesh.shape["gy"]

    def shards(head_old, soil_class, ksat_table, alpha_table, capacity_table, rain, lake_level, pit_id):
        lz, rows, width = head_old.shape
        cells = lz * rows
        f32 = jnp.float32
        block = pltpu.VMEM((cells, width), f32)
        padded = pltpu.VMEM((cells + 2 * rows, width), f32)
        vmem = pl.BlockSpec(memory_space=pltpu.VMEM)
        hbm = pl.BlockSpec(memory_space=pltpu.HBM)
        n = nx * ny
        shapes = (
            jax.ShapeDtypeStruct((cells, width), f32),
            jax.ShapeDtypeStruct((rows, width), f32),
            jax.ShapeDtypeStruct((1, NPIT), f32),
        )
        results = pl.pallas_call(
            functools.partial(kernel, nx, ny, lz, rows),
            out_shape=shapes,
            in_specs=[hbm] * 8,
            out_specs=(vmem, vmem, vmem),
            scratch_shapes=[
                pltpu.SMEM(ksat_table.shape, f32), pltpu.SMEM(ksat_table.shape, f32), pltpu.SMEM(ksat_table.shape, f32),
                pltpu.VMEM((rows, width), f32), pltpu.VMEM((1, NPIT), f32), pltpu.VMEM((rows, width), jnp.int32),
                padded, pltpu.VMEM((cells, width), jnp.int32), padded, block, block, block, padded,
                block, padded, block, padded, pltpu.VMEM((128, rows * 128), f32),
                pltpu.VMEM((2, 2, lz, width), f32), pltpu.VMEM((2, 2, lz, width), f32),
                pltpu.VMEM((2, 2, cells), f32), pltpu.VMEM((2, 2, cells), f32),
                pltpu.VMEM((2, lz, width), f32), pltpu.VMEM((2, lz, width), f32),
                pltpu.VMEM((2, 1, cells), f32), pltpu.VMEM((2, 1, cells), f32),
                pltpu.VMEM((2, lz, width), f32), pltpu.VMEM((2, lz, width), f32),
                pltpu.VMEM((2, 1, cells), f32), pltpu.VMEM((2, 1, cells), f32),
                pltpu.VMEM((n, 8, 128), f32),
                pltpu.SemaphoreType.DMA((8,)),
                pltpu.SemaphoreType.DMA((12,)), pltpu.SemaphoreType.DMA((12,)),
                pltpu.SemaphoreType.DMA((n,)), pltpu.SemaphoreType.DMA((n,)),
            ],
            compiler_params=pltpu.CompilerParams(
                collective_id=0, has_side_effects=True, vmem_limit_bytes=16 * 1024 * 1024
            ),
            name="step",
        )(
            *(pltpu.with_memory_space_constraint(x, pltpu.HBM) for x in (
                head_old.reshape(cells, width), soil_class.reshape(cells, width),
                ksat_table, alpha_table, capacity_table, rain, lake_level.reshape(1, NPIT), pit_id,
            ))
        )
        out, boundary, lake_new = results
        return out.reshape(lz, rows, width), boundary, lake_new.reshape(NPIT)

    return jax.shard_map(
        shards,
        mesh=mesh,
        in_specs=(
            P("scen", "gx", "gy"),
            P(None, "gx", "gy"),
            P(),
            P(),
            P(),
            P(("scen", "gx"), "gy"),
            P("scen"),
            P("gx", "gy"),
        ),
        out_specs=(P("scen", "gx", "gy"), P(("scen", "gx"), "gy"), P("scen")),
        check_vma=False,
    )
```

```python
import functools

import jax
import jax.numpy as jnp
from jax import lax
from jax.experimental import pallas as pl
from jax.experimental.pallas import tpu as pltpu
from jax.sharding import PartitionSpec as P

NPIT = 64
LEAK = 0.5
VERT = 2.0
CH = 20
MESH = pl.DeviceIdType.MESH


def harmonic(first, second):
    return 2.0 * first * second / (first + second)


def kernel(
    nx, ny, lz, rows,
    head_hbm, soil_hbm, ksat_hbm, alpha_hbm, cap_hbm, rain_hbm, lake_hbm, pit_hbm,
    out_ref, bnd_ref, lake_out_ref,
    ksat_ref, alpha_ref, cap_ref, rain_ref, lake_ref, pit_ref, H, SC, C, DG, TX, TY, TZ, R, Z, NZ, U,
    xs1, xr1, ys1, yr1, xs2, xr2, ys2, yr2, xs3, xr3, ys3, yr3,
    gather,
    local_sem, send_sem, recv_sem, ar_send, ar_recv,
):
    f32 = jnp.float32
    mx, my = lax.axis_index("gx"), lax.axis_index("gy")
    n = nx * ny
    me = mx * ny + my
    cells = lz * rows
    lo_pad = rows
    step_rows = CH * rows
    steps = lz // CH

    in_h = pltpu.make_async_copy(head_hbm, H.at[pl.ds(lo_pad, cells)], local_sem.at[0])
    in_s = pltpu.make_async_copy(soil_hbm, SC, local_sem.at[1])
    small = [
        pltpu.make_async_copy(src, dst, local_sem.at[2 + i])
        for i, (src, dst) in enumerate((
            (ksat_hbm, ksat_ref), (alpha_hbm, alpha_ref), (cap_hbm, cap_ref),
            (rain_hbm, rain_ref), (lake_hbm, lake_ref), (pit_hbm, pit_ref),
        ))
    ]
    for each in small[:3] + [in_s, in_h] + small[3:]:
        each.start()

    def peer(s):
        other = lax.rem(me + s, n)
        return {"gx": lax.div(other, ny), "gy": lax.rem(other, ny)}

    def each_peer(body):
        if n <= 16:
            for s in range(1, n):
                body(s)
        else:
            lax.fori_loop(1, n, lambda s, c: (body(s), c)[1], 0)

    barrier = pltpu.get_barrier_semaphore()
    each_peer(lambda s: pl.semaphore_signal(barrier, inc=1, device_id=peer(s), device_id_type=MESH))

    has = {("x", 0): mx > 0, ("x", 1): mx < nx - 1, ("y", 0): my > 0, ("y", 1): my < ny - 1}
    dev = {
        ("x", 0): {"gx": jnp.maximum(mx - 1, 0)},
        ("x", 1): {"gx": jnp.minimum(mx + 1, nx - 1)},
        ("y", 0): {"gy": jnp.maximum(my - 1, 0)},
        ("y", 1): {"gy": jnp.minimum(my + 1, ny - 1)},
    }

    def copy(ax, side, src, dst, number):
        return pltpu.make_async_remote_copy(
            src_ref=src.at[side], dst_ref=dst.at[1 - side],
            send_sem=send_sem.at[number + side], recv_sem=recv_sem.at[number + 1 - side],
            device_id=dev[ax, side], device_id_type=MESH,
        )

    def send(ax, src, dst, number, sides=(0, 1)):
        for side in sides:
            @pl.when(has[ax, side])
            def _(side=side):
                copy(ax, side, src, dst, number).start()

    def receive(ax, src, dst, number, sides=(0, 1)):
        for side in sides:
            @pl.when(has[ax, side])
            def _(side=side):
                copy(ax, 1 - side, src, dst, number).wait_recv()

    def sent(ax, src, dst, number, sides=(0, 1)):
        for side in sides:
            @pl.when(has[ax, side])
            def _(side=side):
                copy(ax, side, src, dst, number).wait_send()

    for ax, buf in (("x", xr1), ("y", yr1), ("x", xr2), ("y", yr2)):
        for side in (0, 1):
            @pl.when(jnp.logical_not(has[ax, side]))
            def _(buf=buf, side=side):
                buf[side] = jnp.zeros(buf.shape[1:], f32)
    for ax, buf in (("x", xr3), ("y", yr3)):
        @pl.when(jnp.logical_not(has[ax, 1]))
        def _(buf=buf):
            buf[1] = jnp.zeros(buf.shape[1:], f32)

    for ref in (H, C, Z, U):
        ref[pl.ds(0, rows), :] = jnp.zeros((rows, 128), f32)
        ref[pl.ds(lo_pad + cells, rows), :] = jnp.zeros((rows, 128), f32)
    TZ[pl.ds(0, rows), :] = jnp.zeros((rows, 128), f32)

    def at(k, shift=0):
        return pl.ds(pl.multiple_of(lo_pad + k * step_rows + shift * rows, rows), step_rows)

    def at0(k):
        return pl.ds(pl.multiple_of(k * step_rows, rows), step_rows)

    for each in small[:3]:
        each.wait()
    in_s.wait()
    in_h.wait()

    @pl.loop(0, steps)
    def _(k):
        classes = SC[at0(k), :]
        ks = jnp.zeros(classes.shape, f32)
        al = jnp.zeros(classes.shape, f32)
        cp = jnp.zeros(classes.shape, f32)
        for which in range(ksat_ref.shape[0]):
            match = classes == which
            ks = jnp.where(match, ksat_ref[which], ks)
            al = jnp.where(match, alpha_ref[which], al)
            cp = jnp.where(match, cap_ref[which], cp)
        relative = jnp.exp(al * jnp.minimum(H[at(k), :], 0.0))
        C[at(k), :] = ks * relative
        DG[at0(k), :] = cp * relative

    def edge(ref, which, pad):
        return ref[pl.ds(pad + which, lz, stride=rows), :]

    c_first, c_last = edge(C, 0, lo_pad), edge(C, rows - 1, lo_pad)
    h_first, h_last = edge(H, 0, lo_pad), edge(H, rows - 1, lo_pad)
    xs1[0, 0], xs1[0, 1] = c_first, h_first
    xs1[1, 0], xs1[1, 1] = c_last, h_last

    def columns(ref, pad):
        turned = ref[pl.ds(pad, cells), :].T
        return turned[0:1, :], turned[127:128, :]

    def to_block(low, high):
        r = lax.broadcasted_iota(jnp.int32, (8, cells), 0)
        top = jnp.where(r == 0, low, f32(0))
        bottom = jnp.where(r == 7, high, f32(0))
        return jnp.concatenate([top, jnp.zeros((112, cells), f32), bottom], axis=0).T

    pl.semaphore_wait(barrier, n - 1)
    send("x", xs1, xr1, 0)
    cy = columns(C, lo_pad)
    hy = columns(H, lo_pad)
    for side in (0, 1):
        ys1[side, 0:1, :] = cy[side]
        ys1[side, 1:2, :] = hy[side]
    send("y", ys1, yr1, 2)

    shape3 = (CH, rows, 128)
    lane = lax.broadcasted_iota(jnp.int32, shape3, 2)
    sub = lax.broadcasted_iota(jnp.int32, shape3, 1)

    def rx(v, s):
        return pltpu.roll(v, s % rows, 1)

    def ry(v, s):
        return pltpu.roll(v, s % 128, 2)

    def get(ref, k, shift=0):
        return ref[at(k, shift), :].reshape(shape3)

    def get0(ref, k):
        return ref[at0(k), :].reshape(shape3)

    def put0(ref, k, v):
        ref[at0(k), :] = v.reshape(step_rows, 128)

    def put(ref, k, v):
        ref[at(k), :] = v.reshape(step_rows, 128)

    @pl.loop(0, steps)
    def _(k):
        c, h = get(C, k), get(H, k)
        tx = jnp.where(sub == rows - 1, 0.0, harmonic(c, rx(c, -1)))
        ty = jnp.where(lane == 127, 0.0, harmonic(c, ry(c, -1)))
        tz = VERT * harmonic(c, get(C, k, 1))
        put0(TX, k, tx)
        put0(TY, k, ty)
        put(TZ, k, tz)
        fx = tx * (rx(h, -1) - h)
        fy = ty * (ry(h, -1) - h)
        fz = tz * (get(H, k, 1) - h)
        tz_low = get(TZ, k, -1)
        fz_low = tz_low * (h - get(H, k, -1))
        put0(DG, k, get0(DG, k) + tx + rx(tx, 1) + ty + ry(ty, 1) + tz + tz_low)
        put0(R, k, fx - rx(fx, 1) + fy - ry(fy, 1) + fz - fz_low)

    for each in small[3:]:
        each.wait()
    pit = pit_ref[...]
    ids = lax.broadcasted_iota(jnp.int32, (NPIT, 128), 0)

    def spread(row):
        column = jnp.broadcast_to(row, (128, 128)).T[:NPIT, :]
        return jnp.concatenate([
            jnp.sum(jnp.where(ids == pit[i:i + 1, :], column, f32(0)), axis=0, keepdims=True)
            for i in range(rows)
        ], axis=0)

    def by_pit(first_field, second_field):
        one, two = jnp.zeros((NPIT, 128), f32), jnp.zeros((NPIT, 128), f32)
        for i in range(rows):
            hit = ids == pit[i:i + 1, :]
            one = one + jnp.where(hit, first_field[i:i + 1, :], f32(0))
            two = two + jnp.where(hit, second_field[i:i + 1, :], f32(0))
        return jnp.sum(jnp.concatenate([one, two], axis=0).T, axis=0, keepdims=True)

    inpit = pit < NPIT
    lake_row = lake_ref[...]
    lake_wide = jnp.concatenate([lake_row, jnp.zeros((1, 128 - NPIT), f32)], axis=1)
    lake_cell = spread(lake_wide)
    top_h = H[pl.ds(lo_pad, rows), :]
    rain = rain_ref[...]
    top_rows = pl.ds(0, rows)
    DG[top_rows, :] += jnp.where(inpit, f32(LEAK), f32(0))
    R[top_rows, :] += rain + jnp.where(inpit, LEAK * (lake_cell - top_h), f32(0))
    rain_area = by_pit(rain, jnp.ones((rows, 128), f32))

    receive("x", xs1, xr1, 0)
    tx_low = harmonic(c_first, xr1[0, 0])
    tx_high = harmonic(c_last, xr1[1, 0])
    first = pl.ds(0, lz, stride=rows)
    last = pl.ds(rows - 1, lz, stride=rows)
    DG[first, :] += tx_low
    DG[last, :] += tx_high
    R[first, :] += tx_low * (xr1[0, 1] - h_first)
    R[last, :] += tx_high * (xr1[1, 1] - h_last)
    receive("y", ys1, yr1, 2)
    ty_low = harmonic(cy[0], yr1[0, 0:1, :])
    ty_high = harmonic(cy[1], yr1[1, 0:1, :])
    NZ[...] = to_block(ty_low, ty_high)
    U[pl.ds(lo_pad, cells), :] = to_block(
        ty_low * (yr1[0, 1:2, :] - hy[0]), ty_high * (yr1[1, 1:2, :] - hy[1])
    )

    zero_acc = jnp.zeros(shape3, f32)

    def make_z(k, acc):
        inverse = 1.0 / (get0(DG, k) + get0(NZ, k))
        r = get0(R, k) + get(U, k)
        z = r * inverse
        put0(DG, k, inverse)
        put0(R, k, r)
        put(Z, k, z)
        return acc + r * z

    acc_a = lax.fori_loop(0, steps, make_z, zero_acc)

    xs2[0] = edge(Z, 0, lo_pad)
    xs2[1] = edge(Z, rows - 1, lo_pad)
    send("x", xs2, xr2, 4)
    zy = columns(Z, lo_pad)
    for side in (0, 1):
        ys2[side] = zy[side]
    send("y", ys2, yr2, 6)

    @pl.loop(0, steps)
    def _(k):
        z, tx, ty = get(Z, k), get0(TX, k), get0(TY, k)
        out = tx * rx(z, -1) + rx(tx * z, 1)
        out = out + ty * ry(z, -1) + ry(ty * z, 1)
        put0(NZ, k, out + get(TZ, k) * get(Z, k, 1) + get(TZ, k, -1) * get(Z, k, -1))

    z_head = by_pit(Z[pl.ds(lo_pad, rows), :], top_h)

    receive("x", xs2, xr2, 4)
    NZ[first, :] += tx_low * xr2[0]
    NZ[last, :] += tx_high * xr2[1]
    receive("y", ys2, yr2, 6)
    U[pl.ds(lo_pad, cells), :] = to_block(ty_low * yr2[0], ty_high * yr2[1])

    def make_u(k, acc):
        nz = get0(NZ, k) + get(U, k)
        u = nz * get0(DG, k)
        put(U, k, u)
        return acc[0] + get0(R, k) * u, acc[1] + nz * u

    acc_g, acc_c = lax.fori_loop(0, steps, make_u, (zero_acc, zero_acc))

    xs3[0] = edge(U, 0, lo_pad)
    send("x", xs3, xr3, 8, (0,))
    uy = columns(U, lo_pad)
    ys3[0] = uy[0]
    send("y", ys3, yr3, 10, (0,))

    def make_f(k, acc):
        u = get(U, k)
        inner = get0(TX, k) * rx(u, -1) + get0(TY, k) * ry(u, -1) + get(TZ, k) * get(U, k, 1)
        return acc + u * inner

    acc_f = lax.fori_loop(0, steps, make_f, zero_acc)
    top_u = U[pl.ds(lo_pad, rows), :]
    u_sum = by_pit(top_u, jnp.zeros((rows, 128), f32))

    def row_sum(acc):
        return jnp.sum(jnp.sum(acc, axis=0), axis=0, keepdims=True)

    sum_a, sum_g, sum_c, sum_f = row_sum(acc_a), row_sum(acc_g), row_sum(acc_c), row_sum(acc_f)
    u_last = edge(U, rows - 1, lo_pad)
    receive("x", xs3, xr3, 8, (1,))
    sum_f = sum_f + jnp.sum(u_last * tx_high * xr3[1], axis=0, keepdims=True)
    receive("y", ys3, yr3, 10, (1,))
    cross = uy[1] * ty_high * yr3[1]
    for i in range(cells // 128):
        sum_f = sum_f + cross[:, i * 128:(i + 1) * 128]
    sum_f = 2.0 * sum_f

    r1 = lax.broadcasted_iota(jnp.int32, (8, 128), 0)
    l1 = lax.broadcasted_iota(jnp.int32, (8, 128), 1)
    scal = jnp.where(r1 == 0, sum_a, jnp.where(r1 == 1, sum_g, jnp.where(r1 == 2, sum_c, sum_f)))
    scal = scal + pltpu.roll(scal, 64, 1)
    pits = jnp.where(r1 < 2, rain_area, jnp.where(r1 < 4, z_head, u_sum))
    swapped = (r1 == 1) | (r1 == 2)
    pits = jnp.where(swapped, pltpu.roll(pits, 128 - NPIT, 1), pits)
    gather[me] = jnp.where(l1 < NPIT, pits, scal)

    def reduce_copy(s):
        return pltpu.make_async_remote_copy(
            src_ref=gather.at[me], dst_ref=gather.at[me], send_sem=ar_send.at[s], recv_sem=ar_recv.at[me],
            device_id=peer(s), device_id_type=MESH,
        )

    def arrival(s):
        source = lax.rem(me + s, n)
        return pltpu.make_async_remote_copy(
            src_ref=gather.at[source], dst_ref=gather.at[source], send_sem=ar_send.at[s], recv_sem=ar_recv.at[source],
            device_id=peer(s), device_id_type=MESH,
        )

    each_peer(lambda s: reduce_copy(s).start())
    each_peer(lambda s: arrival(s).wait_recv())
    if n <= 16:
        total = gather[0]
        for j in range(1, n):
            total = total + gather[j]
    else:
        total = lax.fori_loop(1, n, lambda j, t: t + gather[j], gather[0])

    scalars = jnp.sum(jnp.where(l1 < NPIT, f32(0), total), axis=1, keepdims=True)
    a, g, c, f = (scalars[i:i + 1, :] for i in range(4))
    b = a - g
    step0 = a / b
    ratio = (a * c - g * g) / (b * b)
    p = ratio - g / b
    step1 = a * ratio / (p * p * b + 2.0 * p * step0 * (g - c) + step0 * step0 * (c - f))
    coef_z = step0 + step1 * p
    coef_u = step1 * step0

    coef_z3, coef_u3 = coef_z.reshape(1, 1, 1), coef_u.reshape(1, 1, 1)

    @pl.loop(0, steps)
    def _(k):
        put0(out_ref, k, get(H, k) + coef_z3 * get(Z, k) + coef_u3 * get(U, k))

    inflow, area = total[0:1, :NPIT], total[1:2, :NPIT]
    top_sum = total[2:3, :NPIT] + coef_z * total[3:4, :NPIT] + coef_u * total[4:5, :NPIT]
    outflow = LEAK * (lake_row * area - top_sum)
    lake_new = lake_row + (inflow - outflow) / jnp.maximum(area, 1.0)
    lake_out_ref[...] = lake_new
    lake_new_cell = spread(jnp.concatenate([lake_new, jnp.zeros((1, 128 - NPIT), f32)], axis=1))
    bnd_ref[...] = jnp.where(inpit, lake_new_cell, out_ref[pl.ds(0, rows), :])

    sent("x", xs1, xr1, 0)
    sent("y", ys1, yr1, 2)
    sent("x", xs2, xr2, 4)
    sent("y", ys2, yr2, 6)
    sent("x", xs3, xr3, 8, (0,))
    sent("y", ys3, yr3, 10, (0,))
    each_peer(lambda s: reduce_copy(s).wait_send())


def write_out(a_ref, b_ref, c_ref, a_out, b_out, c_out, sems):
    pairs = ((a_ref, a_out), (b_ref, b_out), (c_ref, c_out))
    copies = [pltpu.make_async_copy(src, dst, sems.at[i]) for i, (src, dst) in enumerate(pairs)]
    for each in copies:
        each.start()
    for each in copies:
        each.wait()


def solution(mesh):
    nx, ny = mesh.shape["gx"], mesh.shape["gy"]

    def shards(head_old, soil_class, ksat_table, alpha_table, capacity_table, rain, lake_level, pit_id):
        lz, rows, width = head_old.shape
        cells = lz * rows
        f32 = jnp.float32
        block = pltpu.VMEM((cells, width), f32)
        padded = pltpu.VMEM((cells + 2 * rows, width), f32)
        vmem = pl.BlockSpec(memory_space=pltpu.VMEM)
        hbm = pl.BlockSpec(memory_space=pltpu.HBM)
        n = nx * ny
        shapes = (
            jax.ShapeDtypeStruct((cells, width), f32),
            jax.ShapeDtypeStruct((rows, width), f32),
            jax.ShapeDtypeStruct((1, NPIT), f32),
        )
        results = pl.pallas_call(
            functools.partial(kernel, nx, ny, lz, rows),
            out_shape=shapes,
            in_specs=[hbm] * 8,
            out_specs=(vmem, vmem, vmem),
            scratch_shapes=[
                pltpu.SMEM(ksat_table.shape, f32), pltpu.SMEM(ksat_table.shape, f32), pltpu.SMEM(ksat_table.shape, f32),
                pltpu.VMEM((rows, width), f32), pltpu.VMEM((1, NPIT), f32), pltpu.VMEM((rows, width), jnp.int32),
                padded, pltpu.VMEM((cells, width), jnp.int32), padded, block, block, block, padded,
                block, padded, block, padded,
                pltpu.VMEM((2, 2, lz, width), f32), pltpu.VMEM((2, 2, lz, width), f32),
                pltpu.VMEM((2, 2, cells), f32), pltpu.VMEM((2, 2, cells), f32),
                pltpu.VMEM((2, lz, width), f32), pltpu.VMEM((2, lz, width), f32),
                pltpu.VMEM((2, 1, cells), f32), pltpu.VMEM((2, 1, cells), f32),
                pltpu.VMEM((2, lz, width), f32), pltpu.VMEM((2, lz, width), f32),
                pltpu.VMEM((2, 1, cells), f32), pltpu.VMEM((2, 1, cells), f32),
                pltpu.VMEM((n, 8, 128), f32),
                pltpu.SemaphoreType.DMA((8,)),
                pltpu.SemaphoreType.DMA((12,)), pltpu.SemaphoreType.DMA((12,)),
                pltpu.SemaphoreType.DMA((n,)), pltpu.SemaphoreType.DMA((n,)),
            ],
            compiler_params=pltpu.CompilerParams(
                collective_id=0, has_side_effects=True, vmem_limit_bytes=16 * 1024 * 1024
            ),
            name="step",
        )(
            *(pltpu.with_memory_space_constraint(x, pltpu.HBM) for x in (
                head_old.reshape(cells, width), soil_class.reshape(cells, width),
                ksat_table, alpha_table, capacity_table, rain, lake_level.reshape(1, NPIT), pit_id,
            ))
        )
        out, boundary, lake_new = pl.pallas_call(
            write_out,
            out_shape=shapes,
            in_specs=[vmem] * 3,
            out_specs=(hbm,) * 3,
            scratch_shapes=[pltpu.SemaphoreType.DMA((3,))],
            name="write",
        )(*(pltpu.with_memory_space_constraint(x, pltpu.VMEM) for x in results))
        return out.reshape(lz, rows, width), boundary, lake_new.reshape(NPIT)

    return jax.shard_map(
        shards,
        mesh=mesh,
        in_specs=(
            P("scen", "gx", "gy"),
            P(None, "gx", "gy"),
            P(),
            P(),
            P(),
            P(("scen", "gx"), "gy"),
            P("scen"),
            P("gx", "gy"),
        ),
        out_specs=(P("scen", "gx", "gy"), P(("scen", "gx"), "gy"), P("scen")),
        check_vma=False,
    )
```

```python
import functools

import jax
import jax.numpy as jnp
from jax import lax
from jax.experimental import pallas as pl
from jax.experimental.pallas import tpu as pltpu
from jax.sharding import PartitionSpec as P

NPIT = 64
LEAK = 0.5
VERT = 2.0
CH = 40
MESH = pl.DeviceIdType.MESH


def harmonic(first, second):
    return 2.0 * first * second / (first + second)


def kernel(
    nx, ny, lz, rows,
    head_hbm, soil_hbm, ksat_hbm, alpha_hbm, cap_hbm, rain_hbm, lake_hbm, pit_hbm,
    out_ref, bnd_ref, lake_out_ref,
    ksat_ref, alpha_ref, cap_ref, rain_ref, lake_ref, pit_ref, H, SC, C, DG, TX, TY, TZ, R, Z, NZ, U,
    xs1, xr1, ys1, yr1, xs2, xr2, ys2, yr2, xs3, xr3, ys3, yr3,
    gather,
    local_sem, send_sem, recv_sem, ar_send, ar_recv,
):
    f32 = jnp.float32
    mx, my = lax.axis_index("gx"), lax.axis_index("gy")
    n = nx * ny
    me = mx * ny + my
    cells = lz * rows
    lo_pad = rows
    step_rows = CH * rows
    steps = lz // CH

    in_h = pltpu.make_async_copy(head_hbm, H.at[pl.ds(lo_pad, cells)], local_sem.at[0])
    in_s = pltpu.make_async_copy(soil_hbm, SC, local_sem.at[1])
    small = [
        pltpu.make_async_copy(src, dst, local_sem.at[2 + i])
        for i, (src, dst) in enumerate((
            (ksat_hbm, ksat_ref), (alpha_hbm, alpha_ref), (cap_hbm, cap_ref),
            (rain_hbm, rain_ref), (lake_hbm, lake_ref), (pit_hbm, pit_ref),
        ))
    ]
    for each in small[:3] + [in_s, in_h] + small[3:]:
        each.start()

    def peer(s):
        other = lax.rem(me + s, n)
        return {"gx": lax.div(other, ny), "gy": lax.rem(other, ny)}

    def each_peer(body):
        if n <= 16:
            for s in range(1, n):
                body(s)
        else:
            lax.fori_loop(1, n, lambda s, c: (body(s), c)[1], 0)

    barrier = pltpu.get_barrier_semaphore()
    each_peer(lambda s: pl.semaphore_signal(barrier, inc=1, device_id=peer(s), device_id_type=MESH))

    has = {("x", 0): mx > 0, ("x", 1): mx < nx - 1, ("y", 0): my > 0, ("y", 1): my < ny - 1}
    dev = {
        ("x", 0): {"gx": jnp.maximum(mx - 1, 0)},
        ("x", 1): {"gx": jnp.minimum(mx + 1, nx - 1)},
        ("y", 0): {"gy": jnp.maximum(my - 1, 0)},
        ("y", 1): {"gy": jnp.minimum(my + 1, ny - 1)},
    }

    def copy(ax, side, src, dst, number):
        return pltpu.make_async_remote_copy(
            src_ref=src.at[side], dst_ref=dst.at[1 - side],
            send_sem=send_sem.at[number + side], recv_sem=recv_sem.at[number + 1 - side],
            device_id=dev[ax, side], device_id_type=MESH,
        )

    def send(ax, src, dst, number, sides=(0, 1)):
        for side in sides:
            @pl.when(has[ax, side])
            def _(side=side):
                copy(ax, side, src, dst, number).start()

    def receive(ax, src, dst, number, sides=(0, 1)):
        for side in sides:
            @pl.when(has[ax, side])
            def _(side=side):
                copy(ax, 1 - side, src, dst, number).wait_recv()

    def sent(ax, src, dst, number, sides=(0, 1)):
        for side in sides:
            @pl.when(has[ax, side])
            def _(side=side):
                copy(ax, side, src, dst, number).wait_send()

    for ax, buf in (("x", xr1), ("y", yr1), ("x", xr2), ("y", yr2)):
        for side in (0, 1):
            @pl.when(jnp.logical_not(has[ax, side]))
            def _(buf=buf, side=side):
                buf[side] = jnp.zeros(buf.shape[1:], f32)
    for ax, buf in (("x", xr3), ("y", yr3)):
        @pl.when(jnp.logical_not(has[ax, 1]))
        def _(buf=buf):
            buf[1] = jnp.zeros(buf.shape[1:], f32)

    for ref in (H, C, Z, U):
        ref[pl.ds(0, rows), :] = jnp.zeros((rows, 128), f32)
        ref[pl.ds(lo_pad + cells, rows), :] = jnp.zeros((rows, 128), f32)
    TZ[pl.ds(0, rows), :] = jnp.zeros((rows, 128), f32)

    def at(k, shift=0):
        return pl.ds(pl.multiple_of(lo_pad + k * step_rows + shift * rows, rows), step_rows)

    def at0(k):
        return pl.ds(pl.multiple_of(k * step_rows, rows), step_rows)

    for each in small[:3]:
        each.wait()
    in_s.wait()
    in_h.wait()

    def soil(classes, head):
        ks = jnp.zeros(classes.shape, f32)
        al = jnp.zeros(classes.shape, f32)
        cp = jnp.zeros(classes.shape, f32)
        for which in range(ksat_ref.shape[0]):
            match = classes == which
            ks = jnp.where(match, ksat_ref[which], ks)
            al = jnp.where(match, alpha_ref[which], al)
            cp = jnp.where(match, cap_ref[which], cp)
        relative = jnp.exp(al * jnp.minimum(head, 0.0))
        return ks * relative, cp * relative

    def edge(ref, which, pad):
        return ref[pl.ds(pad + which, lz, stride=rows), :]

    h_first, h_last = edge(H, 0, lo_pad), edge(H, rows - 1, lo_pad)
    c_first, _ = soil(edge(SC, 0, 0), h_first)
    c_last, _ = soil(edge(SC, rows - 1, 0), h_last)
    xs1[0, 0], xs1[0, 1] = c_first, h_first
    xs1[1, 0], xs1[1, 1] = c_last, h_last
    pl.semaphore_wait(barrier, n - 1)
    send("x", xs1, xr1, 0)

    @pl.loop(0, steps)
    def _(k):
        cond, store = soil(SC[at0(k), :], H[at(k), :])
        C[at(k), :] = cond
        DG[at0(k), :] = store

    def columns(ref, pad):
        turned = ref[pl.ds(pad, cells), :].T
        return turned[0:1, :], turned[127:128, :]

    def to_block(low, high):
        r = lax.broadcasted_iota(jnp.int32, (8, cells), 0)
        top = jnp.where(r == 0, low, f32(0))
        bottom = jnp.where(r == 7, high, f32(0))
        return jnp.concatenate([top, jnp.zeros((112, cells), f32), bottom], axis=0).T

    cy = columns(C, lo_pad)
    hy = columns(H, lo_pad)
    for side in (0, 1):
        ys1[side, 0:1, :] = cy[side]
        ys1[side, 1:2, :] = hy[side]
    send("y", ys1, yr1, 2)

    shape3 = (CH, rows, 128)
    lane = lax.broadcasted_iota(jnp.int32, shape3, 2)
    sub = lax.broadcasted_iota(jnp.int32, shape3, 1)

    def rx(v, s):
        return pltpu.roll(v, s % rows, 1)

    def ry(v, s):
        return pltpu.roll(v, s % 128, 2)

    def get(ref, k, shift=0):
        return ref[at(k, shift), :].reshape(shape3)

    def get0(ref, k):
        return ref[at0(k), :].reshape(shape3)

    def put0(ref, k, v):
        ref[at0(k), :] = v.reshape(step_rows, 128)

    def put(ref, k, v):
        ref[at(k), :] = v.reshape(step_rows, 128)

    @pl.loop(0, steps)
    def _(k):
        c, h = get(C, k), get(H, k)
        tx = jnp.where(sub == rows - 1, 0.0, harmonic(c, rx(c, -1)))
        ty = jnp.where(lane == 127, 0.0, harmonic(c, ry(c, -1)))
        tz = VERT * harmonic(c, get(C, k, 1))
        put0(TX, k, tx)
        put0(TY, k, ty)
        put(TZ, k, tz)
        fx = tx * (rx(h, -1) - h)
        fy = ty * (ry(h, -1) - h)
        fz = tz * (get(H, k, 1) - h)
        tz_low = get(TZ, k, -1)
        fz_low = tz_low * (h - get(H, k, -1))
        put0(DG, k, get0(DG, k) + tx + rx(tx, 1) + ty + ry(ty, 1) + tz + tz_low)
        put0(R, k, fx - rx(fx, 1) + fy - ry(fy, 1) + fz - fz_low)

    for each in small[3:]:
        each.wait()
    pit = pit_ref[...]
    ids = lax.broadcasted_iota(jnp.int32, (NPIT, 128), 0)

    def spread(row):
        column = jnp.broadcast_to(row, (128, 128)).T[:NPIT, :]
        return jnp.concatenate([
            jnp.sum(jnp.where(ids == pit[i:i + 1, :], column, f32(0)), axis=0, keepdims=True)
            for i in range(rows)
        ], axis=0)

    def by_pit(first_field, second_field):
        one, two = jnp.zeros((NPIT, 128), f32), jnp.zeros((NPIT, 128), f32)
        for i in range(rows):
            hit = ids == pit[i:i + 1, :]
            one = one + jnp.where(hit, first_field[i:i + 1, :], f32(0))
            two = two + jnp.where(hit, second_field[i:i + 1, :], f32(0))
        return jnp.sum(jnp.concatenate([one, two], axis=0).T, axis=0, keepdims=True)

    inpit = pit < NPIT
    lake_row = lake_ref[...]
    lake_wide = jnp.concatenate([lake_row, jnp.zeros((1, 128 - NPIT), f32)], axis=1)
    lake_cell = spread(lake_wide)
    top_h = H[pl.ds(lo_pad, rows), :]
    rain = rain_ref[...]
    top_rows = pl.ds(0, rows)
    DG[top_rows, :] += jnp.where(inpit, f32(LEAK), f32(0))
    R[top_rows, :] += rain + jnp.where(inpit, LEAK * (lake_cell - top_h), f32(0))
    rain_area = by_pit(rain, jnp.ones((rows, 128), f32))

    receive("x", xs1, xr1, 0)
    tx_low = harmonic(c_first, xr1[0, 0])
    tx_high = harmonic(c_last, xr1[1, 0])
    first = pl.ds(0, lz, stride=rows)
    last = pl.ds(rows - 1, lz, stride=rows)
    DG[first, :] += tx_low
    DG[last, :] += tx_high
    R[first, :] += tx_low * (xr1[0, 1] - h_first)
    R[last, :] += tx_high * (xr1[1, 1] - h_last)
    receive("y", ys1, yr1, 2)
    ty_low = harmonic(cy[0], yr1[0, 0:1, :])
    ty_high = harmonic(cy[1], yr1[1, 0:1, :])
    NZ[...] = to_block(ty_low, ty_high)
    U[pl.ds(lo_pad, cells), :] = to_block(
        ty_low * (yr1[0, 1:2, :] - hy[0]), ty_high * (yr1[1, 1:2, :] - hy[1])
    )

    for side, row in ((0, 0), (1, rows - 1)):
        inverse_row = 1.0 / (edge(DG, row, 0) + edge(NZ, row, 0))
        xs2[side] = (edge(R, row, 0) + edge(U, row, lo_pad)) * inverse_row
    send("x", xs2, xr2, 4)

    zero_acc = jnp.zeros(shape3, f32)

    def make_z(k, acc):
        inverse = 1.0 / (get0(DG, k) + get0(NZ, k))
        r = get0(R, k) + get(U, k)
        z = r * inverse
        put0(DG, k, inverse)
        put0(R, k, r)
        put(Z, k, z)
        return acc + r * z

    acc_a = lax.fori_loop(0, steps, make_z, zero_acc)

    zy = columns(Z, lo_pad)
    for side in (0, 1):
        ys2[side] = zy[side]
    send("y", ys2, yr2, 6)

    @pl.loop(0, steps)
    def _(k):
        z, tx, ty = get(Z, k), get0(TX, k), get0(TY, k)
        out = tx * rx(z, -1) + rx(tx * z, 1)
        out = out + ty * ry(z, -1) + ry(ty * z, 1)
        put0(NZ, k, out + get(TZ, k) * get(Z, k, 1) + get(TZ, k, -1) * get(Z, k, -1))

    z_head = by_pit(Z[pl.ds(lo_pad, rows), :], top_h)

    receive("x", xs2, xr2, 4)
    NZ[first, :] += tx_low * xr2[0]
    NZ[last, :] += tx_high * xr2[1]
    receive("y", ys2, yr2, 6)
    U[pl.ds(lo_pad, cells), :] = to_block(ty_low * yr2[0], ty_high * yr2[1])

    xs3[0] = (edge(NZ, 0, 0) + edge(U, 0, lo_pad)) * edge(DG, 0, 0)
    send("x", xs3, xr3, 8, (0,))

    def make_u(k, acc):
        nz = get0(NZ, k) + get(U, k)
        u = nz * get0(DG, k)
        put(U, k, u)
        return acc[0] + get0(R, k) * u, acc[1] + nz * u

    acc_g, acc_c = lax.fori_loop(0, steps, make_u, (zero_acc, zero_acc))

    uy = columns(U, lo_pad)
    ys3[0] = uy[0]
    send("y", ys3, yr3, 10, (0,))

    def make_f(k, acc):
        u = get(U, k)
        inner = get0(TX, k) * rx(u, -1) + get0(TY, k) * ry(u, -1) + get(TZ, k) * get(U, k, 1)
        return acc + u * inner

    acc_f = lax.fori_loop(0, steps, make_f, zero_acc)
    top_u = U[pl.ds(lo_pad, rows), :]
    u_sum = by_pit(top_u, jnp.zeros((rows, 128), f32))

    def row_sum(acc):
        return jnp.sum(jnp.sum(acc, axis=0), axis=0, keepdims=True)

    sum_a, sum_g, sum_c, sum_f = row_sum(acc_a), row_sum(acc_g), row_sum(acc_c), row_sum(acc_f)
    u_last = edge(U, rows - 1, lo_pad)
    receive("x", xs3, xr3, 8, (1,))
    sum_f = sum_f + jnp.sum(u_last * tx_high * xr3[1], axis=0, keepdims=True)
    receive("y", ys3, yr3, 10, (1,))
    cross = uy[1] * ty_high * yr3[1]
    for i in range(cells // 128):
        sum_f = sum_f + cross[:, i * 128:(i + 1) * 128]
    sum_f = 2.0 * sum_f

    r1 = lax.broadcasted_iota(jnp.int32, (8, 128), 0)
    l1 = lax.broadcasted_iota(jnp.int32, (8, 128), 1)
    scal = jnp.where(r1 == 0, sum_a, jnp.where(r1 == 1, sum_g, jnp.where(r1 == 2, sum_c, sum_f)))
    scal = scal + pltpu.roll(scal, 64, 1)
    pits = jnp.where(r1 < 2, rain_area, jnp.where(r1 < 4, z_head, u_sum))
    swapped = (r1 == 1) | (r1 == 2)
    pits = jnp.where(swapped, pltpu.roll(pits, 128 - NPIT, 1), pits)
    gather[me] = jnp.where(l1 < NPIT, pits, scal)

    def reduce_copy(s):
        return pltpu.make_async_remote_copy(
            src_ref=gather.at[me], dst_ref=gather.at[me], send_sem=ar_send.at[s], recv_sem=ar_recv.at[me],
            device_id=peer(s), device_id_type=MESH,
        )

    def arrival(s):
        source = lax.rem(me + s, n)
        return pltpu.make_async_remote_copy(
            src_ref=gather.at[source], dst_ref=gather.at[source], send_sem=ar_send.at[s], recv_sem=ar_recv.at[source],
            device_id=peer(s), device_id_type=MESH,
        )

    each_peer(lambda s: reduce_copy(s).start())
    each_peer(lambda s: arrival(s).wait_recv())
    if n <= 16:
        total = gather[0]
        for j in range(1, n):
            total = total + gather[j]
    else:
        total = lax.fori_loop(1, n, lambda j, t: t + gather[j], gather[0])

    scalars = jnp.sum(jnp.where(l1 < NPIT, f32(0), total), axis=1, keepdims=True)
    a, g, c, f = (scalars[i:i + 1, :] for i in range(4))
    b = a - g
    step0 = a / b
    ratio = (a * c - g * g) / (b * b)
    p = ratio - g / b
    step1 = a * ratio / (p * p * b + 2.0 * p * step0 * (g - c) + step0 * step0 * (c - f))
    coef_z = step0 + step1 * p
    coef_u = step1 * step0

    coef_z3, coef_u3 = coef_z.reshape(1, 1, 1), coef_u.reshape(1, 1, 1)

    @pl.loop(0, steps)
    def _(k):
        put0(out_ref, k, get(H, k) + coef_z3 * get(Z, k) + coef_u3 * get(U, k))

    inflow, area = total[0:1, :NPIT], total[1:2, :NPIT]
    top_sum = total[2:3, :NPIT] + coef_z * total[3:4, :NPIT] + coef_u * total[4:5, :NPIT]
    outflow = LEAK * (lake_row * area - top_sum)
    lake_new = lake_row + (inflow - outflow) / jnp.maximum(area, 1.0)
    lake_out_ref[...] = lake_new
    lake_new_cell = spread(jnp.concatenate([lake_new, jnp.zeros((1, 128 - NPIT), f32)], axis=1))
    bnd_ref[...] = jnp.where(inpit, lake_new_cell, out_ref[pl.ds(0, rows), :])

    sent("x", xs1, xr1, 0)
    sent("y", ys1, yr1, 2)
    sent("x", xs2, xr2, 4)
    sent("y", ys2, yr2, 6)
    sent("x", xs3, xr3, 8, (0,))
    sent("y", ys3, yr3, 10, (0,))
    each_peer(lambda s: reduce_copy(s).wait_send())


def write_out(a_ref, b_ref, c_ref, a_out, b_out, c_out, sems):
    pairs = ((a_ref, a_out), (b_ref, b_out), (c_ref, c_out))
    copies = [pltpu.make_async_copy(src, dst, sems.at[i]) for i, (src, dst) in enumerate(pairs)]
    for each in copies:
        each.start()
    for each in copies:
        each.wait()


def solution(mesh):
    nx, ny = mesh.shape["gx"], mesh.shape["gy"]

    def shards(head_old, soil_class, ksat_table, alpha_table, capacity_table, rain, lake_level, pit_id):
        lz, rows, width = head_old.shape
        cells = lz * rows
        f32 = jnp.float32
        block = pltpu.VMEM((cells, width), f32)
        padded = pltpu.VMEM((cells + 2 * rows, width), f32)
        vmem = pl.BlockSpec(memory_space=pltpu.VMEM)
        hbm = pl.BlockSpec(memory_space=pltpu.HBM)
        n = nx * ny
        shapes = (
            jax.ShapeDtypeStruct((cells, width), f32),
            jax.ShapeDtypeStruct((rows, width), f32),
            jax.ShapeDtypeStruct((1, NPIT), f32),
        )
        results = pl.pallas_call(
            functools.partial(kernel, nx, ny, lz, rows),
            out_shape=shapes,
            in_specs=[hbm] * 8,
            out_specs=(vmem, vmem, vmem),
            scratch_shapes=[
                pltpu.SMEM(ksat_table.shape, f32), pltpu.SMEM(ksat_table.shape, f32), pltpu.SMEM(ksat_table.shape, f32),
                pltpu.VMEM((rows, width), f32), pltpu.VMEM((1, NPIT), f32), pltpu.VMEM((rows, width), jnp.int32),
                padded, pltpu.VMEM((cells, width), jnp.int32), padded, block, block, block, padded,
                block, padded, block, padded,
                pltpu.VMEM((2, 2, lz, width), f32), pltpu.VMEM((2, 2, lz, width), f32),
                pltpu.VMEM((2, 2, cells), f32), pltpu.VMEM((2, 2, cells), f32),
                pltpu.VMEM((2, lz, width), f32), pltpu.VMEM((2, lz, width), f32),
                pltpu.VMEM((2, 1, cells), f32), pltpu.VMEM((2, 1, cells), f32),
                pltpu.VMEM((2, lz, width), f32), pltpu.VMEM((2, lz, width), f32),
                pltpu.VMEM((2, 1, cells), f32), pltpu.VMEM((2, 1, cells), f32),
                pltpu.VMEM((n, 8, 128), f32),
                pltpu.SemaphoreType.DMA((8,)),
                pltpu.SemaphoreType.DMA((12,)), pltpu.SemaphoreType.DMA((12,)),
                pltpu.SemaphoreType.DMA((n,)), pltpu.SemaphoreType.DMA((n,)),
            ],
            compiler_params=pltpu.CompilerParams(
                collective_id=0, has_side_effects=True, vmem_limit_bytes=16 * 1024 * 1024
            ),
            name="step",
        )(
            *(pltpu.with_memory_space_constraint(x, pltpu.HBM) for x in (
                head_old.reshape(cells, width), soil_class.reshape(cells, width),
                ksat_table, alpha_table, capacity_table, rain, lake_level.reshape(1, NPIT), pit_id,
            ))
        )
        out, boundary, lake_new = pl.pallas_call(
            write_out,
            out_shape=shapes,
            in_specs=[vmem] * 3,
            out_specs=(hbm,) * 3,
            scratch_shapes=[pltpu.SemaphoreType.DMA((3,))],
            name="write",
        )(*(pltpu.with_memory_space_constraint(x, pltpu.VMEM) for x in results))
        return out.reshape(lz, rows, width), boundary, lake_new.reshape(NPIT)

    return jax.shard_map(
        shards,
        mesh=mesh,
        in_specs=(
            P("scen", "gx", "gy"),
            P(None, "gx", "gy"),
            P(),
            P(),
            P(),
            P(("scen", "gx"), "gy"),
            P("scen"),
            P("gx", "gy"),
        ),
        out_specs=(P("scen", "gx", "gy"), P(("scen", "gx"), "gy"), P("scen")),
        check_vma=False,
    )
```

```python
import functools

import jax
import jax.numpy as jnp
from jax import lax
from jax.experimental import pallas as pl
from jax.experimental.pallas import tpu as pltpu
from jax.sharding import PartitionSpec as P

NPIT = 64
LEAK = 0.5
VERT = 2.0
CH = 40
MESH = pl.DeviceIdType.MESH


def harmonic(first, second):
    return 2.0 * first * second / (first + second)


def kernel(
    nx, ny, lz, rows,
    head_hbm, soil_hbm, ksat_hbm, alpha_hbm, cap_hbm, rain_hbm, lake_hbm, pit_hbm,
    out_ref, bnd_ref, lake_out_ref,
    ksat_ref, alpha_ref, cap_ref, rain_ref, lake_ref, pit_ref, H, SC, C, DG, TX, TY, TZ, R, Z, NZ, U,
    xs1, xr1, ys1, yr1, xs2, xr2, ys2, yr2, xs3, xr3, ys3, yr3,
    gather,
    local_sem, send_sem, recv_sem, ar_send, ar_recv,
):
    f32 = jnp.float32
    mx, my = lax.axis_index("gx"), lax.axis_index("gy")
    n = nx * ny
    me = mx * ny + my
    cells = lz * rows
    lo_pad = rows
    step_rows = CH * rows
    steps = lz // CH

    in_h = pltpu.make_async_copy(head_hbm, H.at[pl.ds(lo_pad, cells)], local_sem.at[0])
    in_s = pltpu.make_async_copy(soil_hbm, SC, local_sem.at[1])
    small = [
        pltpu.make_async_copy(src, dst, local_sem.at[2 + i])
        for i, (src, dst) in enumerate((
            (ksat_hbm, ksat_ref), (alpha_hbm, alpha_ref), (cap_hbm, cap_ref),
            (rain_hbm, rain_ref), (lake_hbm, lake_ref), (pit_hbm, pit_ref),
        ))
    ]
    for each in small[:3] + [in_s, in_h] + small[3:]:
        each.start()

    def peer(s):
        other = lax.rem(me + s, n)
        return {"gx": lax.div(other, ny), "gy": lax.rem(other, ny)}

    def each_peer(body):
        if n <= 16:
            for s in range(1, n):
                body(s)
        else:
            lax.fori_loop(1, n, lambda s, c: (body(s), c)[1], 0)

    barrier = pltpu.get_barrier_semaphore()
    each_peer(lambda s: pl.semaphore_signal(barrier, inc=1, device_id=peer(s), device_id_type=MESH))

    has = {("x", 0): mx > 0, ("x", 1): mx < nx - 1, ("y", 0): my > 0, ("y", 1): my < ny - 1}
    dev = {
        ("x", 0): {"gx": jnp.maximum(mx - 1, 0)},
        ("x", 1): {"gx": jnp.minimum(mx + 1, nx - 1)},
        ("y", 0): {"gy": jnp.maximum(my - 1, 0)},
        ("y", 1): {"gy": jnp.minimum(my + 1, ny - 1)},
    }

    def copy(ax, side, src, dst, number):
        return pltpu.make_async_remote_copy(
            src_ref=src.at[side], dst_ref=dst.at[1 - side],
            send_sem=send_sem.at[number + side], recv_sem=recv_sem.at[number + 1 - side],
            device_id=dev[ax, side], device_id_type=MESH,
        )

    def send(ax, src, dst, number, sides=(0, 1)):
        for side in sides:
            @pl.when(has[ax, side])
            def _(side=side):
                copy(ax, side, src, dst, number).start()

    def receive(ax, src, dst, number, sides=(0, 1)):
        for side in sides:
            @pl.when(has[ax, side])
            def _(side=side):
                copy(ax, 1 - side, src, dst, number).wait_recv()

    def sent(ax, src, dst, number, sides=(0, 1)):
        for side in sides:
            @pl.when(has[ax, side])
            def _(side=side):
                copy(ax, side, src, dst, number).wait_send()

    for ax, buf in (("x", xr1), ("y", yr1), ("x", xr2), ("y", yr2)):
        for side in (0, 1):
            @pl.when(jnp.logical_not(has[ax, side]))
            def _(buf=buf, side=side):
                buf[side] = jnp.zeros(buf.shape[1:], f32)
    for ax, buf in (("x", xr3), ("y", yr3)):
        @pl.when(jnp.logical_not(has[ax, 1]))
        def _(buf=buf):
            buf[1] = jnp.zeros(buf.shape[1:], f32)

    for ref in (H, C, Z, U):
        ref[pl.ds(0, rows), :] = jnp.zeros((rows, 128), f32)
        ref[pl.ds(lo_pad + cells, rows), :] = jnp.zeros((rows, 128), f32)
    TZ[pl.ds(0, rows), :] = jnp.zeros((rows, 128), f32)

    def at(k, shift=0):
        return pl.ds(pl.multiple_of(lo_pad + k * step_rows + shift * rows, rows), step_rows)

    def at0(k):
        return pl.ds(pl.multiple_of(k * step_rows, rows), step_rows)

    for each in small[:3]:
        each.wait()
    in_s.wait()
    in_h.wait()

    def soil(classes, head):
        ks = jnp.zeros(classes.shape, f32)
        al = jnp.zeros(classes.shape, f32)
        cp = jnp.zeros(classes.shape, f32)
        for which in range(ksat_ref.shape[0]):
            match = classes == which
            ks = jnp.where(match, ksat_ref[which], ks)
            al = jnp.where(match, alpha_ref[which], al)
            cp = jnp.where(match, cap_ref[which], cp)
        relative = jnp.exp(al * jnp.minimum(head, 0.0))
        return ks * relative, cp * relative

    def edge(ref, which, pad):
        return ref[pl.ds(pad + which, lz, stride=rows), :]

    h_first, h_last = edge(H, 0, lo_pad), edge(H, rows - 1, lo_pad)
    c_first, _ = soil(edge(SC, 0, 0), h_first)
    c_last, _ = soil(edge(SC, rows - 1, 0), h_last)
    xs1[0, 0], xs1[0, 1] = c_first, h_first
    xs1[1, 0], xs1[1, 1] = c_last, h_last
    pl.semaphore_wait(barrier, n - 1)
    send("x", xs1, xr1, 0)

    @pl.loop(0, steps)
    def _(k):
        cond, store = soil(SC[at0(k), :], H[at(k), :])
        C[at(k), :] = cond
        DG[at0(k), :] = store

    def columns(ref, pad):
        turned = ref[pl.ds(pad, cells), :].T
        return turned[0:1, :], turned[127:128, :]

    def to_block(low, high):
        r = lax.broadcasted_iota(jnp.int32, (8, cells), 0)
        top = jnp.where(r == 0, low, f32(0))
        bottom = jnp.where(r == 7, high, f32(0))
        return jnp.concatenate([top, jnp.zeros((112, cells), f32), bottom], axis=0).T

    cy = columns(C, lo_pad)
    hy = columns(H, lo_pad)
    for side in (0, 1):
        ys1[side, 0:1, :] = cy[side]
        ys1[side, 1:2, :] = hy[side]
    send("y", ys1, yr1, 2)

    shape3 = (CH, rows, 128)
    lane = lax.broadcasted_iota(jnp.int32, shape3, 2)
    sub = lax.broadcasted_iota(jnp.int32, shape3, 1)

    def rx(v, s):
        return pltpu.roll(v, s % rows, 1)

    def ry(v, s):
        return pltpu.roll(v, s % 128, 2)

    def get(ref, k, shift=0):
        return ref[at(k, shift), :].reshape(shape3)

    def get0(ref, k):
        return ref[at0(k), :].reshape(shape3)

    def put0(ref, k, v):
        ref[at0(k), :] = v.reshape(step_rows, 128)

    def put(ref, k, v):
        ref[at(k), :] = v.reshape(step_rows, 128)

    @pl.loop(0, steps)
    def _(k):
        c, h = get(C, k), get(H, k)
        tx = jnp.where(sub == rows - 1, 0.0, harmonic(c, rx(c, -1)))
        ty = jnp.where(lane == 127, 0.0, harmonic(c, ry(c, -1)))
        tz = VERT * harmonic(c, get(C, k, 1))
        put0(TX, k, tx)
        put0(TY, k, ty)
        put(TZ, k, tz)
        fx = tx * (rx(h, -1) - h)
        fy = ty * (ry(h, -1) - h)
        fz = tz * (get(H, k, 1) - h)
        tz_low = get(TZ, k, -1)
        fz_low = tz_low * (h - get(H, k, -1))
        put0(DG, k, get0(DG, k) + tx + rx(tx, 1) + ty + ry(ty, 1) + tz + tz_low)
        put0(R, k, fx - rx(fx, 1) + fy - ry(fy, 1) + fz - fz_low)

    for each in small[3:]:
        each.wait()
    pit = pit_ref[...]
    ids = lax.broadcasted_iota(jnp.int32, (NPIT, 128), 0)

    def spread(row):
        column = jnp.broadcast_to(row, (128, 128)).T[:NPIT, :]
        return jnp.concatenate([
            jnp.sum(jnp.where(ids == pit[i:i + 1, :], column, f32(0)), axis=0, keepdims=True)
            for i in range(rows)
        ], axis=0)

    def by_pit(first_field, second_field):
        one, two = jnp.zeros((NPIT, 128), f32), jnp.zeros((NPIT, 128), f32)
        for i in range(rows):
            hit = ids == pit[i:i + 1, :]
            one = one + jnp.where(hit, first_field[i:i + 1, :], f32(0))
            two = two + jnp.where(hit, second_field[i:i + 1, :], f32(0))
        return jnp.sum(jnp.concatenate([one, two], axis=0).T, axis=0, keepdims=True)

    inpit = pit < NPIT
    lake_row = lake_ref[...]
    lake_wide = jnp.concatenate([lake_row, jnp.zeros((1, 128 - NPIT), f32)], axis=1)
    lake_cell = spread(lake_wide)
    top_h = H[pl.ds(lo_pad, rows), :]
    rain = rain_ref[...]
    top_rows = pl.ds(0, rows)
    DG[top_rows, :] += jnp.where(inpit, f32(LEAK), f32(0))
    R[top_rows, :] += rain + jnp.where(inpit, LEAK * (lake_cell - top_h), f32(0))
    supply_area = by_pit(rain + LEAK * top_h, jnp.ones((rows, 128), f32))

    receive("x", xs1, xr1, 0)
    tx_low = harmonic(c_first, xr1[0, 0])
    tx_high = harmonic(c_last, xr1[1, 0])
    first = pl.ds(0, lz, stride=rows)
    last = pl.ds(rows - 1, lz, stride=rows)
    DG[first, :] += tx_low
    DG[last, :] += tx_high
    R[first, :] += tx_low * (xr1[0, 1] - h_first)
    R[last, :] += tx_high * (xr1[1, 1] - h_last)
    receive("y", ys1, yr1, 2)
    ty_low = harmonic(cy[0], yr1[0, 0:1, :])
    ty_high = harmonic(cy[1], yr1[1, 0:1, :])
    NZ[...] = to_block(ty_low, ty_high)
    U[pl.ds(lo_pad, cells), :] = to_block(
        ty_low * (yr1[0, 1:2, :] - hy[0]), ty_high * (yr1[1, 1:2, :] - hy[1])
    )

    for side, row in ((0, 0), (1, rows - 1)):
        inverse_row = 1.0 / (edge(DG, row, 0) + edge(NZ, row, 0))
        xs2[side] = (edge(R, row, 0) + edge(U, row, lo_pad)) * inverse_row
    send("x", xs2, xr2, 4)

    zero_acc = jnp.zeros(shape3, f32)

    def make_z(k, acc):
        inverse = 1.0 / (get0(DG, k) + get0(NZ, k))
        r = get0(R, k) + get(U, k)
        z = r * inverse
        put0(DG, k, inverse)
        put0(R, k, r)
        put(Z, k, z)
        return acc + r * z

    acc_a = lax.fori_loop(0, steps, make_z, zero_acc)

    zy = columns(Z, lo_pad)
    for side in (0, 1):
        ys2[side] = zy[side]
    send("y", ys2, yr2, 6)

    @pl.loop(0, steps)
    def _(k):
        z, tx, ty = get(Z, k), get0(TX, k), get0(TY, k)
        out = tx * rx(z, -1) + rx(tx * z, 1)
        out = out + ty * ry(z, -1) + ry(ty * z, 1)
        put0(NZ, k, out + get(TZ, k) * get(Z, k, 1) + get(TZ, k, -1) * get(Z, k, -1))

    z_sum = by_pit(Z[pl.ds(lo_pad, rows), :], jnp.zeros((rows, 128), f32))

    receive("x", xs2, xr2, 4)
    NZ[first, :] += tx_low * xr2[0]
    NZ[last, :] += tx_high * xr2[1]
    receive("y", ys2, yr2, 6)
    U[pl.ds(lo_pad, cells), :] = to_block(ty_low * yr2[0], ty_high * yr2[1])

    xs3[0] = (edge(NZ, 0, 0) + edge(U, 0, lo_pad)) * edge(DG, 0, 0)
    send("x", xs3, xr3, 8, (0,))

    def make_u(k, acc):
        nz = get0(NZ, k) + get(U, k)
        u = nz * get0(DG, k)
        put(U, k, u)
        return acc[0] + get0(R, k) * u, acc[1] + nz * u

    acc_g, acc_c = lax.fori_loop(0, steps, make_u, (zero_acc, zero_acc))

    uy = columns(U, lo_pad)
    ys3[0] = uy[0]
    send("y", ys3, yr3, 10, (0,))

    def make_f(k, acc):
        u = get(U, k)
        inner = get0(TX, k) * rx(u, -1) + get0(TY, k) * ry(u, -1) + get(TZ, k) * get(U, k, 1)
        return acc + u * inner

    acc_f = lax.fori_loop(0, steps, make_f, zero_acc)
    top_u = U[pl.ds(lo_pad, rows), :]
    u_sum = by_pit(top_u, jnp.zeros((rows, 128), f32))

    def row_sum(acc):
        return jnp.sum(jnp.sum(acc, axis=0), axis=0, keepdims=True)

    sum_a, sum_g, sum_c, sum_f = row_sum(acc_a), row_sum(acc_g), row_sum(acc_c), row_sum(acc_f)
    u_last = edge(U, rows - 1, lo_pad)
    receive("x", xs3, xr3, 8, (1,))
    sum_f = sum_f + jnp.sum(u_last * tx_high * xr3[1], axis=0, keepdims=True)
    receive("y", ys3, yr3, 10, (1,))
    cross = uy[1] * ty_high * yr3[1]
    for i in range(cells // 128):
        sum_f = sum_f + cross[:, i * 128:(i + 1) * 128]
    sum_f = 2.0 * sum_f

    half = lax.broadcasted_iota(jnp.int32, (1, 128), 1) < NPIT

    def fold(row):
        return row + pltpu.roll(row, 64, 1)

    gather[me, 0:1, :] = supply_area
    gather[me, 1:2, :] = jnp.where(half, z_sum, fold(sum_a))
    gather[me, 2:3, :] = jnp.where(half, u_sum, fold(sum_g))
    gather[me, 3:4, :] = jnp.where(half, fold(sum_c), fold(sum_f))

    def reduce_copy(s):
        return pltpu.make_async_remote_copy(
            src_ref=gather.at[me], dst_ref=gather.at[me], send_sem=ar_send.at[s], recv_sem=ar_recv.at[me],
            device_id=peer(s), device_id_type=MESH,
        )

    def arrival(s):
        source = lax.rem(me + s, n)
        return pltpu.make_async_remote_copy(
            src_ref=gather.at[source], dst_ref=gather.at[source], send_sem=ar_send.at[s], recv_sem=ar_recv.at[source],
            device_id=peer(s), device_id_type=MESH,
        )

    each_peer(lambda s: reduce_copy(s).start())
    each_peer(lambda s: arrival(s).wait_recv())
    if n <= 16:
        total = gather[0]
        for j in range(1, n):
            total = total + gather[j]
    else:
        total = lax.fori_loop(1, n, lambda j, t: t + gather[j], gather[0])

    def half_sum(row, low):
        return jnp.sum(jnp.where(half == low, row, f32(0)), axis=1, keepdims=True)

    a, g = half_sum(total[1:2, :], False), half_sum(total[2:3, :], False)
    c, f = half_sum(total[3:4, :], True), half_sum(total[3:4, :], False)
    b = a - g
    step0 = a / b
    ratio = (a * c - g * g) / (b * b)
    p = ratio - g / b
    step1 = a * ratio / (p * p * b + 2.0 * p * step0 * (g - c) + step0 * step0 * (c - f))
    coef_z = step0 + step1 * p
    coef_u = step1 * step0

    coef_z3, coef_u3 = coef_z.reshape(1, 1, 1), coef_u.reshape(1, 1, 1)

    @pl.loop(0, steps)
    def _(k):
        put0(out_ref, k, get(H, k) + coef_z3 * get(Z, k) + coef_u3 * get(U, k))

    supply = total[0:1, :NPIT]
    area = pltpu.roll(total, 64, 1)[0:1, :NPIT]
    change = coef_z * total[1:2, :NPIT] + coef_u * total[2:3, :NPIT]
    lake_new = lake_row + (supply + LEAK * (change - lake_row * area)) / jnp.maximum(area, 1.0)
    lake_out_ref[...] = lake_new
    lake_new_cell = spread(jnp.concatenate([lake_new, jnp.zeros((1, 128 - NPIT), f32)], axis=1))
    bnd_ref[...] = jnp.where(inpit, lake_new_cell, out_ref[pl.ds(0, rows), :])

    sent("x", xs1, xr1, 0)
    sent("y", ys1, yr1, 2)
    sent("x", xs2, xr2, 4)
    sent("y", ys2, yr2, 6)
    sent("x", xs3, xr3, 8, (0,))
    sent("y", ys3, yr3, 10, (0,))
    each_peer(lambda s: reduce_copy(s).wait_send())


def write_out(a_ref, b_ref, c_ref, a_out, b_out, c_out, sems):
    pairs = ((a_ref, a_out), (b_ref, b_out), (c_ref, c_out))
    copies = [pltpu.make_async_copy(src, dst, sems.at[i]) for i, (src, dst) in enumerate(pairs)]
    for each in copies:
        each.start()
    for each in copies:
        each.wait()


def solution(mesh):
    nx, ny = mesh.shape["gx"], mesh.shape["gy"]

    def shards(head_old, soil_class, ksat_table, alpha_table, capacity_table, rain, lake_level, pit_id):
        lz, rows, width = head_old.shape
        cells = lz * rows
        f32 = jnp.float32
        block = pltpu.VMEM((cells, width), f32)
        padded = pltpu.VMEM((cells + 2 * rows, width), f32)
        vmem = pl.BlockSpec(memory_space=pltpu.VMEM)
        hbm = pl.BlockSpec(memory_space=pltpu.HBM)
        n = nx * ny
        shapes = (
            jax.ShapeDtypeStruct((cells, width), f32),
            jax.ShapeDtypeStruct((rows, width), f32),
            jax.ShapeDtypeStruct((1, NPIT), f32),
        )
        results = pl.pallas_call(
            functools.partial(kernel, nx, ny, lz, rows),
            out_shape=shapes,
            in_specs=[hbm] * 8,
            out_specs=(vmem, vmem, vmem),
            scratch_shapes=[
                pltpu.SMEM(ksat_table.shape, f32), pltpu.SMEM(ksat_table.shape, f32), pltpu.SMEM(ksat_table.shape, f32),
                pltpu.VMEM((rows, width), f32), pltpu.VMEM((1, NPIT), f32), pltpu.VMEM((rows, width), jnp.int32),
                padded, pltpu.VMEM((cells, width), jnp.int32), padded, block, block, block, padded,
                block, padded, block, padded,
                pltpu.VMEM((2, 2, lz, width), f32), pltpu.VMEM((2, 2, lz, width), f32),
                pltpu.VMEM((2, 2, cells), f32), pltpu.VMEM((2, 2, cells), f32),
                pltpu.VMEM((2, lz, width), f32), pltpu.VMEM((2, lz, width), f32),
                pltpu.VMEM((2, 1, cells), f32), pltpu.VMEM((2, 1, cells), f32),
                pltpu.VMEM((2, lz, width), f32), pltpu.VMEM((2, lz, width), f32),
                pltpu.VMEM((2, 1, cells), f32), pltpu.VMEM((2, 1, cells), f32),
                pltpu.VMEM((n, 4, 128), f32),
                pltpu.SemaphoreType.DMA((8,)),
                pltpu.SemaphoreType.DMA((12,)), pltpu.SemaphoreType.DMA((12,)),
                pltpu.SemaphoreType.DMA((n,)), pltpu.SemaphoreType.DMA((n,)),
            ],
            compiler_params=pltpu.CompilerParams(
                collective_id=0, has_side_effects=True, vmem_limit_bytes=16 * 1024 * 1024
            ),
            name="step",
        )(
            *(pltpu.with_memory_space_constraint(x, pltpu.HBM) for x in (
                head_old.reshape(cells, width), soil_class.reshape(cells, width),
                ksat_table, alpha_table, capacity_table, rain, lake_level.reshape(1, NPIT), pit_id,
            ))
        )
        out, boundary, lake_new = pl.pallas_call(
            write_out,
            out_shape=shapes,
            in_specs=[vmem] * 3,
            out_specs=(hbm,) * 3,
            scratch_shapes=[pltpu.SemaphoreType.DMA((3,))],
            name="write",
        )(*(pltpu.with_memory_space_constraint(x, pltpu.VMEM) for x in results))
        return out.reshape(lz, rows, width), boundary, lake_new.reshape(NPIT)

    return jax.shard_map(
        shards,
        mesh=mesh,
        in_specs=(
            P("scen", "gx", "gy"),
            P(None, "gx", "gy"),
            P(),
            P(),
            P(),
            P(("scen", "gx"), "gy"),
            P("scen"),
            P("gx", "gy"),
        ),
        out_specs=(P("scen", "gx", "gy"), P(("scen", "gx"), "gy"), P("scen")),
        check_vma=False,
    )
```
